128 devices in a mesh: facet: 16 (over x, y), sub: 8 (over z, core).
Axes of the slice: x: 4, y: 4, z: 4, core: 2. Of those that a mesh axis runs over, the one named last changes fastest.
Arguments:
- facet_spec: bfloat16 [16, 2, 1216, 704], P('facet'), may hold values from -3 to 3
- worker_of_subgrid: int32 [128], replicated, may hold values from 0 to 127, each once
- vis_count: int32 [128], P(('facet', 'sub')), may hold values from 512 to 8192, as said below
- bin_offsets: int32 [128, 2, 8192], P(('facet', 'sub')), may hold values from 0 to 248
- bin_fractions: float32 [128, 2, 8192], P(('facet', 'sub')), may hold values from 0 to 1
- observed: float32 [128, 2, 8192], P(('facet', 'sub')), may hold values from -6 to 6
Outputs:
- residual_vis: float32 [128, 2, 8192], P(('facet', 'sub'))
- facet_update: float32 [16, 2, 1216, 704], P('facet', None, 'sub')
The draws below stay inside these ranges and needn't reach their ends.
Inputs may be any that keep to these rules, and one draw needn't show every extreme that they name: `worker_of_subgrid`: a permutation of the subgrids. `vis_count`: some device row has all 8192 slots live in every draw.
All inputs are finite; a program needn't handle non-finite values.
Results may differ from the reference program's by a relative error of at most 0.014.
Values may be sent and summed in bfloat16 or wider, within the bound.
No kernel may reach another device: no remote copies, remote signals or barrier semaphores. Data moves between devices by JAX's collectives and lax.ppermute only.
A program may use at most 128 MiB of HBM per device.

```python
import math
import jax
import jax.numpy as jnp
from jax import lax

SUB = 256
MC = 256
STEP = 64
KS = 8
VMAX = 8192
POS_V = 8
FACETS = 16
SUBGRIDS = 128
PR = 1216
PC = 704


def draw_vis_count(key, part):
    low_key = jax.random.fold_in(key, 11)
    crowd_key = jax.random.fold_in(key, 12)
    pick_key = jax.random.fold_in(key, 13)
    base = jax.random.randint(low_key, (SUBGRIDS,), VMAX // 16, VMAX // 2 + 1)
    crowded = jax.random.randint(crowd_key, (SUBGRIDS,), 0, 8) == 0
    chosen = jax.random.randint(pick_key, (), 0, SUBGRIDS)
    crowded = crowded | (jnp.arange(SUBGRIDS) == chosen)
    return jnp.where(crowded, VMAX, base).astype(jnp.int32)


def set_ends(entries, own_key, least, largest):
    spot = [jax.random.randint(jax.random.fold_in(own_key, axis), (), 0, length) for axis, length in enumerate(entries.shape)]
    main_axis = entries.shape.index(max(entries.shape))
    next_to = spot[:main_axis] + [(spot[main_axis] + 1) % entries.shape[main_axis]] + spot[main_axis + 1:]
    return entries.at[tuple(spot)].set(least).at[tuple(next_to)].set(largest)


def shard_levels(key, dims, split, smallest, largest):
    def one(dim, parts):
        heights = jax.random.uniform(jax.random.fold_in(jax.random.fold_in(key, 6), dim), (parts,), jnp.float32, smallest / len(split), largest / len(split))
        return jnp.repeat(jnp.exp(heights), dims[dim] // parts).reshape((-1,) + (1,) * (len(dims) - dim - 1))

    gain = one(*split[0])
    for cut in split[1:]:
        gain = gain * one(*cut)
    return gain


def scatter_about(key, extent, spread, most, pieces=(), kind=jnp.bfloat16):
    values = spread * jax.random.normal(key, extent, jnp.float32)
    if pieces:
        values = values * shard_levels(key, extent, pieces, -0.22, 0.18)
    return jnp.clip(values, -most, most).astype(kind)


def setup_inputs(seed: int = 0) -> dict:
    arg_keys = jax.random.split(jax.random.key(seed), 7)
    facet_spec = scatter_about(arg_keys[0], (FACETS, 2, PR, PC), 0.5, 3.0, ((0, 16),))
    worker_of_subgrid = jax.random.permutation(arg_keys[1], SUBGRIDS).astype(jnp.int32)
    vis_count = draw_vis_count(jax.random.fold_in(arg_keys[6], 71), 0)
    bin_offsets = set_ends(jax.random.randint(arg_keys[3], (SUBGRIDS, 2, VMAX), 0, SUB - KS + 1), jax.random.fold_in(arg_keys[3], 1), 0, SUB - KS).astype(jnp.int32)
    bin_fractions = jnp.clip(1.0 * jax.random.uniform(arg_keys[4], (SUBGRIDS, 2, VMAX), jnp.float32) ** shard_levels(arg_keys[4], (SUBGRIDS, 2, VMAX), ((0, 128),), -0.2, 0.2), 0.0, 1.0)
    observed = scatter_about(arg_keys[5], (SUBGRIDS, 2, VMAX), 1.0, 6.0, ((0, 128),), jnp.float32)
    return dict(facet_spec=facet_spec, worker_of_subgrid=worker_of_subgrid, vis_count=vis_count, bin_offsets=bin_offsets, bin_fractions=bin_fractions, observed=observed)


TWO_PI = 2.0 * math.pi


def phase_table(offset, facets, swapped, conj_sign):
    sub_index = jnp.arange(SUB, dtype=jnp.int32) - SUB // 2
    win_index = jnp.arange(MC, dtype=jnp.int32) - MC // 2
    if swapped:
        sub_part = sub_index[None, :]
        win_part = win_index[:, None]
    else:
        sub_part = sub_index[:, None]
        win_part = win_index[None, :]
    modulus = SUB * facets
    residue = jnp.mod(sub_part * win_part * facets + sub_part * offset, modulus)
    angles = residue.astype(jnp.float32) * (TWO_PI / modulus)
    factor = MC ** -0.5
    return jnp.stack([jnp.cos(angles) * factor, conj_sign * jnp.sin(angles) * factor]).astype(jnp.bfloat16)


def wide_dot(first_part, second_part):
    return jnp.dot(first_part.astype(jnp.float32), second_part.astype(jnp.float32), precision=lax.Precision.HIGHEST, preferred_element_type=jnp.float32)


def pair_dot(first_pair, second_pair):
    real_real = wide_dot(first_pair[0], second_pair[0])
    imag_imag = wide_dot(first_pair[1], second_pair[1])
    real_imag = wide_dot(first_pair[0], second_pair[1])
    imag_real = wide_dot(first_pair[1], second_pair[0])
    return jnp.stack([real_real - imag_imag, real_imag + imag_real])


def kernel_rows(offsets, fractions):
    cells = jnp.arange(SUB, dtype=jnp.int32)[None, :] - offsets[:, None]
    distance = cells.astype(jnp.float32) - fractions[:, None] - (0.5 * KS - 1.0)
    inside = (cells >= 0) & (cells < KS)
    weights = jnp.where(inside, 0.5 * jnp.exp(-jnp.square(distance * (9.0 / KS))), 0.0)
    return weights.astype(jnp.bfloat16)


def subgrid_holder(worker):
    total_rows = worker.shape[0]
    slot_ids = jnp.arange(total_rows, dtype=jnp.int32)
    matches = (worker[None, :] == slot_ids[:, None]).astype(jnp.int32)
    return jnp.sum(matches * slot_ids[None, :], axis=1).astype(jnp.int32)


def adjoint_window(resid_grid, facet_id, facets):
    left_table = phase_table(facet_id, facets, True, -1.0)
    right_table = phase_table(jnp.mod(5 * facet_id + 3, facets), facets, False, -1.0)
    partial_value = pair_dot(left_table, resid_grid).astype(jnp.bfloat16)
    return pair_dot(partial_value, right_table).astype(jnp.bfloat16)


def reference(facet_spec, worker_of_subgrid, vis_count, bin_offsets, bin_fractions, observed):
    facets = facet_spec.shape[0]
    holder = subgrid_holder(worker_of_subgrid)
    facet_ids = jnp.arange(facets, dtype=jnp.int32)
    anchor = jnp.int32(0)

    def device_row(planes, device_id):
        subgrid = holder[device_id]
        top_row = ((subgrid // POS_V) * STEP).astype(jnp.int32)
        left_col = ((subgrid % POS_V) * STEP).astype(jnp.int32)

        def add_facet(running, facet_id):
            contribution = lax.dynamic_slice(facet_spec, (facet_id, anchor, top_row, left_col), (1, 2, MC, MC))[0]
            left_table = phase_table(facet_id, facets, False, 1.0)
            right_table = phase_table(jnp.mod(5 * facet_id + 3, facets), facets, True, 1.0)
            partial_value = pair_dot(left_table, contribution).astype(jnp.bfloat16)
            return running + pair_dot(partial_value, right_table), None

        grid_sum, _ = lax.scan(add_facet, jnp.zeros((2, SUB, SUB), jnp.float32), facet_ids)
        grid_half = grid_sum.astype(jnp.bfloat16)
        grid_cat = jnp.concatenate([grid_half[0], grid_half[1]], axis=1)
        offsets = bin_offsets[device_id]
        fractions = bin_fractions[device_id]
        observed_rows = observed[device_id]
        u_weights = kernel_rows(offsets[0], fractions[0])
        v_weights = kernel_rows(offsets[1], fractions[1])
        product = wide_dot(u_weights, grid_cat)
        v_float = v_weights.astype(jnp.float32)
        model_real = jnp.sum(product[:, :SUB] * v_float, axis=1)
        model_imag = jnp.sum(product[:, SUB:] * v_float, axis=1)
        live_mask = jnp.arange(VMAX, dtype=jnp.int32) < vis_count[device_id]
        real_part = jnp.where(live_mask, observed_rows[0] - model_real, 0.0)
        imag_part = jnp.where(live_mask, observed_rows[1] - model_imag, 0.0)
        weighted = jnp.concatenate([real_part[:, None] * v_float, imag_part[:, None] * v_float], axis=1).astype(jnp.bfloat16)
        gridded = lax.dot_general(u_weights.astype(jnp.float32), weighted.astype(jnp.float32), (((0,), (0,)), ((), ())), precision=lax.Precision.HIGHEST, preferred_element_type=jnp.float32)
        resid_grid = jnp.stack([gridded[:, :SUB], gridded[:, SUB:]]).astype(jnp.bfloat16)

        def one_window(facet_id):
            return adjoint_window(resid_grid, facet_id, facets)

        windows = lax.map(one_window, facet_ids)
        current = lax.dynamic_slice(planes, (anchor, anchor, top_row, left_col), (facets, 2, MC, MC))
        planes = lax.dynamic_update_slice(planes, current + windows.astype(jnp.float32), (anchor, anchor, top_row, left_col))
        return planes, jnp.stack([real_part, imag_part])

    planes, residual = lax.scan(device_row, jnp.zeros((facets, 2, PR, PC), jnp.float32), jnp.arange(SUBGRIDS, dtype=jnp.int32))
    return residual, planes
```

```python
import math

import jax
import jax.numpy as jnp
import numpy as np
from jax import lax
from jax.experimental import pallas as pl
from jax.experimental.pallas import tpu as pltpu
from jax.sharding import PartitionSpec as P

SUB = 256
MC = 256
STEP = 64
KS = 8
BLOCK = 1024
LANES = 128
MIB = 1 << 20


def phase_tables(facets):
    sub_part = (np.arange(SUB) - SUB // 2)[:, None]
    win_part = (np.arange(MC) - MC // 2)[None, :]
    modulus = SUB * facets
    tables = []
    for offset in range(facets):
        residue = np.mod(sub_part * win_part * facets + sub_part * offset, modulus)
        angles = residue.astype(np.float32).astype(np.float64) * (2.0 * math.pi / modulus)
        factor = MC ** (-0.5)
        tables.append(np.stack([np.cos(angles) * factor, np.sin(angles) * factor]))
    return np.stack(tables).astype(jnp.bfloat16)


def side_by_side(first, second):
    return jnp.concatenate([first, second], axis=1)


def stacked(first, second):
    return jnp.concatenate([first, second], axis=0)


def f32_dot(left, right):
    return jnp.dot(left, right, preferred_element_type=jnp.float32)


def contribution_kernel(place, spec, left, right, out, shifted_spec, left_mat, right_mat):
    step = pl.program_id(0)
    reach = shifted_spec.shape[2]

    @pl.when(step == 0)
    def _():
        for part in range(2):
            shifted_spec[part] = spec[0, part, :, STEP : STEP + reach]
        a_re, a_im = left[0, 0], left[0, 1]
        left_mat[...] = stacked(side_by_side(a_re, -a_im), side_by_side(a_im, a_re))
        b_re, b_im = right[0, 0], right[0, 1]
        right_mat[...] = stacked(side_by_side(b_re, b_im), side_by_side(-b_im, b_re))

    top = pl.multiple_of(place[2 + 2 * step], STEP)
    left_step = place[3 + 2 * step]
    col = pl.multiple_of(left_step // 2 * LANES, LANES)

    def finish(window):
        half = f32_dot(left_mat[...], window).astype(jnp.bfloat16)
        whole = f32_dot(side_by_side(half[:SUB], half[SUB:]), right_mat[...])
        out[0, :SUB] = whole[:, :SUB].astype(jnp.bfloat16)
        out[0, SUB:] = whole[:, SUB:].astype(jnp.bfloat16)

    @pl.when(left_step % 2 == 0)
    def _():
        finish(
            stacked(
                spec[0, 0, pl.ds(top, MC), pl.ds(col, MC)],
                spec[0, 1, pl.ds(top, MC), pl.ds(col, MC)],
            )
        )

    @pl.when(left_step % 2 == 1)
    def _():
        finish(
            stacked(
                shifted_spec[0, pl.ds(top, MC), pl.ds(col, MC)],
                shifted_spec[1, pl.ds(top, MC), pl.ds(col, MC)],
            )
        )


def contributions(place, spec, tables, tables_t):
    facets = tables.shape[0]
    rows, cols = spec.shape[2:]
    flops = facets * 2 * 2 * 512 * 512 * 256
    return pl.pallas_call(
        contribution_kernel,
        out_shape=jax.ShapeDtypeStruct((facets, 2 * SUB, SUB), jnp.bfloat16),
        grid_spec=pltpu.PrefetchScalarGridSpec(
            num_scalar_prefetch=1,
            grid=(facets,),
            in_specs=[
                pl.BlockSpec((1, 2, rows, cols), lambda t, place: (0, 0, 0, 0)),
                pl.BlockSpec((1, 2, SUB, MC), lambda t, place: (place[0], 0, 0, 0)),
                pl.BlockSpec((1, 2, MC, SUB), lambda t, place: (place[1], 0, 0, 0)),
            ],
            out_specs=pl.BlockSpec((1, 2 * SUB, SUB), lambda t, place: (t, 0, 0)),
            scratch_shapes=[
                pltpu.VMEM((2, rows, cols - STEP), jnp.bfloat16),
                pltpu.VMEM((2 * SUB, 2 * MC), jnp.bfloat16),
                pltpu.VMEM((2 * MC, 2 * SUB), jnp.bfloat16),
            ],
        ),
        compiler_params=pltpu.CompilerParams(vmem_limit_bytes=32 * MIB),
        cost_estimate=pl.CostEstimate(
            flops=flops, bytes_accessed=8 * MIB, transcendentals=0
        ),
        name="facet_contributions",
    )(place, spec, tables, tables_t)


def weights_kernel(offsets, fractions, u_out, v_out):
    cells = lax.broadcasted_iota(jnp.int32, (SUB, BLOCK), 0).astype(jnp.float32)
    scale = -((9.0 / KS) ** 2) / math.log(2.0)
    for axis, out in enumerate((u_out, v_out)):
        first = offsets[0, axis : axis + 1, :].astype(jnp.float32)
        inside = jnp.abs(cells - (first + 0.5 * (KS - 1))) < 0.5 * KS
        distance = cells - (first + (fractions[0, axis : axis + 1, :] + (0.5 * KS - 1.0)))
        weights = jnp.exp2(distance * distance * scale - 1.0)
        out[...] = jnp.where(inside, weights, 0.0).astype(jnp.bfloat16)


def kernel_weights(offsets, fractions):
    slots = offsets.shape[2]
    block_in = pl.BlockSpec((1, 2, BLOCK), lambda b: (0, 0, b))
    block_out = pl.BlockSpec((SUB, BLOCK), lambda b: (0, b))
    shape = jax.ShapeDtypeStruct((SUB, slots), jnp.bfloat16)
    return pl.pallas_call(
        weights_kernel,
        out_shape=(shape, shape),
        grid=(slots // BLOCK,),
        in_specs=[block_in, block_in],
        out_specs=(block_out, block_out),
        compiler_params=pltpu.CompilerParams(vmem_limit_bytes=32 * MIB),
        cost_estimate=pl.CostEstimate(
            flops=20 * SUB * slots, bytes_accessed=4 * SUB * slots, transcendentals=2 * SUB * slots
        ),
        name="kernel_weights",
    )(offsets, fractions)


def residual_kernel(count, grid_in, u_in, v_in, observed, resid_out, grid_out, total):
    step = pl.program_id(0)

    @pl.when(step == 0)
    def _():
        total[...] = jnp.zeros_like(total)

    u_half = u_in[...]
    v_half = v_in[...]
    product = f32_dot(grid_in[0], v_half)
    u_wide = u_half.astype(jnp.float32)
    v_wide = v_half.astype(jnp.float32)
    slot = step * BLOCK + lax.broadcasted_iota(jnp.int32, (1, BLOCK), 1)
    live = slot < count[0]
    for part in range(2):
        model = jnp.sum(product[part * SUB : (part + 1) * SUB] * u_wide, axis=0, keepdims=True)
        resid = jnp.where(live, observed[0, part : part + 1, :] - model, 0.0)
        resid_out[0, part : part + 1, :] = resid
        weighted = (resid * v_wide).astype(jnp.bfloat16)
        total[part * SUB : (part + 1) * SUB] += lax.dot_general(
            u_half, weighted, (((1,), (1,)), ((), ())), preferred_element_type=jnp.float32
        )

    @pl.when(step == pl.num_programs(0) - 1)
    def _():
        grid_out[...] = total[...].astype(jnp.bfloat16)


def residuals(count, grid, u_weights, v_weights, observed):
    slots = observed.shape[2]
    vis_block = pl.BlockSpec((1, 2, BLOCK), lambda b, count: (0, 0, b))
    weight_block = pl.BlockSpec((SUB, BLOCK), lambda b, count: (0, b))
    return pl.pallas_call(
        residual_kernel,
        out_shape=(
            jax.ShapeDtypeStruct(observed.shape, jnp.float32),
            jax.ShapeDtypeStruct((2 * SUB, SUB), jnp.bfloat16),
        ),
        grid_spec=pltpu.PrefetchScalarGridSpec(
            num_scalar_prefetch=1,
            grid=(slots // BLOCK,),
            in_specs=[
                pl.BlockSpec((1, 2 * SUB, SUB), lambda b, count: (0, 0, 0)),
                weight_block,
                weight_block,
                vis_block,
            ],
            out_specs=(vis_block, pl.BlockSpec((2 * SUB, SUB), lambda b, count: (0, 0))),
            scratch_shapes=[pltpu.VMEM((2 * SUB, SUB), jnp.float32)],
        ),
        compiler_params=pltpu.CompilerParams(vmem_limit_bytes=32 * MIB),
        cost_estimate=pl.CostEstimate(
            flops=4 * 512 * 256 * slots, bytes_accessed=4 * SUB * slots, transcendentals=0
        ),
        name="residuals",
    )(count, grid, u_weights, v_weights, observed)


def adjoint_kernel(place, grids, left, right, out, plane, left_mat, right_mat):
    step = pl.program_id(0)
    bands, _, band_rows, cols = out.shape

    @pl.when(step == 0)
    def _():
        plane[...] = jnp.zeros_like(plane)
        a_re, a_im = left[0, 0], left[0, 1]
        left_mat[...] = stacked(side_by_side(a_re, a_im), side_by_side(-a_im, a_re))
        b_re, b_im = right[0, 0], right[0, 1]
        right_mat[...] = stacked(side_by_side(b_re, -b_im), side_by_side(b_im, b_re))

    top = pl.multiple_of(place[2 + 2 * step], STEP)
    left_step = place[3 + 2 * step]
    col = pl.multiple_of(left_step // 2 * LANES, LANES)
    half = f32_dot(left_mat[...], grids[0]).astype(jnp.bfloat16)
    whole = f32_dot(side_by_side(half[:MC], half[MC:]), right_mat[...])

    @pl.when(left_step % 2 == 0)
    def _():
        for part in range(2):
            plane[part, pl.ds(top, MC), pl.ds(col, MC)] += whole[:, part * MC : (part + 1) * MC]

    @pl.when(left_step % 2 == 1)
    def _():
        edge = jnp.zeros((MC, STEP), jnp.float32)
        for part in range(2):
            plane[part, pl.ds(top, MC), pl.ds(col, MC + LANES)] += jnp.concatenate(
                [edge, whole[:, part * MC : (part + 1) * MC], edge], axis=1
            )

    @pl.when(step == pl.num_programs(0) - 1)
    def _():
        for band in range(bands):
            for part in range(2):
                out[band, part] = plane[
                    part, band * band_rows : (band + 1) * band_rows, :cols
                ].astype(jnp.bfloat16)


def adjoint_plane(place, grids, tables, tables_t, bands, rows, cols):
    facets = tables.shape[0]
    flops = facets * 2 * 2 * 512 * 512 * 256
    wide = (cols + LANES - 1) // LANES * LANES
    return pl.pallas_call(
        adjoint_kernel,
        out_shape=jax.ShapeDtypeStruct((bands, 2, rows // bands, cols), jnp.bfloat16),
        grid_spec=pltpu.PrefetchScalarGridSpec(
            num_scalar_prefetch=1,
            grid=(facets,),
            in_specs=[
                pl.BlockSpec((1, 2 * SUB, SUB), lambda t, place: (t, 0, 0)),
                pl.BlockSpec((1, 2, MC, SUB), lambda t, place: (place[0], 0, 0, 0)),
                pl.BlockSpec((1, 2, SUB, MC), lambda t, place: (place[1], 0, 0, 0)),
            ],
            out_specs=pl.BlockSpec((bands, 2, rows // bands, cols), lambda t, place: (0, 0, 0, 0)),
            scratch_shapes=[
                pltpu.VMEM((2, rows, wide), jnp.float32),
                pltpu.VMEM((2 * MC, 2 * SUB), jnp.bfloat16),
                pltpu.VMEM((2 * SUB, 2 * MC), jnp.bfloat16),
            ],
        ),
        compiler_params=pltpu.CompilerParams(vmem_limit_bytes=40 * MIB),
        cost_estimate=pl.CostEstimate(
            flops=flops, bytes_accessed=8 * MIB, transcendentals=0
        ),
        name="adjoint_plane",
    )(place, grids, tables_t, tables)


def places(worker, facets, subs):
    facet = lax.axis_index("facet")
    rows = jnp.arange(facets, dtype=jnp.int32) * subs + lax.axis_index("sub")
    ids = jnp.arange(worker.shape[0], dtype=jnp.int32)
    held = jnp.sum(jnp.where(worker[None, :] == rows[:, None], ids[None, :], 0), axis=1)
    head = jnp.stack([facet, jnp.mod(5 * facet + 3, facets)]).astype(jnp.int32)
    corners = jnp.stack([held // subs * STEP, held % subs], axis=1)
    return jnp.concatenate([head, corners.reshape(-1)])


def on_device(facet_spec, worker_of_subgrid, vis_count, bin_offsets, bin_fractions, observed):
    facets = lax.axis_size("facet")
    subs = lax.axis_size("sub")
    rows, cols = facet_spec.shape[2:]
    table = phase_tables(facets)
    tables = jnp.asarray(table)
    tables_t = jnp.asarray(np.ascontiguousarray(table.transpose(0, 1, 3, 2)))
    place = places(worker_of_subgrid, facets, subs)
    parts = contributions(place, facet_spec, tables, tables_t)
    u_weights, v_weights = kernel_weights(bin_offsets, bin_fractions)
    grid = lax.psum_scatter(parts, "facet", scatter_dimension=0, tiled=True)
    residual, resid_grid = residuals(vis_count, grid, u_weights, v_weights, observed)
    grids = lax.all_gather(resid_grid, "facet", axis=0, tiled=False)
    plane = adjoint_plane(place, grids, tables, tables_t, subs, rows, cols)
    update = lax.psum_scatter(plane, "sub", scatter_dimension=0, tiled=True)
    return (residual, update.astype(jnp.float32))


def solution(mesh):
    placed = (
        P("facet", None, None, None),
        P(),
        P(("facet", "sub")),
        P(("facet", "sub"), None, None),
        P(("facet", "sub"), None, None),
        P(("facet", "sub"), None, None),
    )
    return jax.shard_map(
        on_device,
        mesh=mesh,
        in_specs=placed,
        out_specs=(P(("facet", "sub"), None, None), P("facet", None, "sub", None)),
        check_vma=False,
    )
```

```python
import math

import jax
import jax.numpy as jnp
import numpy as np
from jax import lax
from jax.experimental import pallas as pl
from jax.experimental.pallas import tpu as pltpu
from jax.sharding import PartitionSpec as P

SUB = 256
MC = 256
STEP = 64
KS = 8
BLOCK = 1024
LANES = 128
HALF = SUB // 2
RING = 4
NEAR = (0, 1, RING - 1, 2)
MIB = 1 << 20
VMEM_LIMIT = 58 * MIB


def phase_tables(facets):
    sub_part = (np.arange(SUB) - SUB // 2)[:, None]
    win_part = (np.arange(MC) - MC // 2)[None, :]
    modulus = SUB * facets
    tables = []
    for offset in range(facets):
        residue = np.mod(sub_part * win_part * facets + sub_part * offset, modulus)
        angles = residue.astype(np.float32).astype(np.float64) * (2.0 * math.pi / modulus)
        factor = MC ** (-0.5)
        tables.append(np.stack([np.cos(angles) * factor, np.sin(angles) * factor]))
    return np.stack(tables).astype(jnp.bfloat16)


def side_by_side(*blocks):
    return jnp.concatenate(blocks, axis=1)


def stacked(*blocks):
    return jnp.concatenate(blocks, axis=0)


def f32_dot(left, right):
    return jnp.dot(left, right, preferred_element_type=jnp.float32)


def contribution_kernel(place, spec, left, right, *rest):
    a_own, a_up, a_down, a_far_up, a_far_down = rest[:5]
    b_own, b_up, b_down, b_far_up, b_far_down = rest[5:10]
    windows, left_mat, right_mat = rest[10:]
    step = pl.program_id(0)
    reach = windows.shape[3]

    @pl.when(step == 0)
    def _():
        for part in range(2):
            windows[0, part] = spec[0, part, :, :reach]
            windows[1, part] = spec[0, part, :, STEP : STEP + reach]
        a_re, a_im = left[0, 0], left[0, 1]
        right_mat[...] = stacked(side_by_side(a_re, a_im), side_by_side(-a_im, a_re))
        b_re, b_im = right[0, 0], right[0, 1]
        left_mat[...] = stacked(side_by_side(b_re, -b_im), side_by_side(b_im, b_re))

    results = []
    for other in range(RING):
        target = step * RING + other
        row_step = place[2 + 2 * target]
        first_col = pl.multiple_of(place[3 + 2 * target], STEP)
        odd = row_step % 2
        first_row = pl.multiple_of(row_step // 2 * LANES, LANES)
        window = side_by_side(
            windows[odd, 0, pl.ds(first_col, MC), pl.ds(first_row, MC)],
            windows[odd, 1, pl.ds(first_col, MC), pl.ds(first_row, MC)],
        )
        half = f32_dot(window, right_mat[...]).astype(jnp.bfloat16)
        whole = f32_dot(left_mat[...], stacked(half[:, :SUB], half[:, SUB:]))
        results.append(whole.astype(jnp.bfloat16))

    for near, out in ((0, a_own), (1, a_up), (2, a_down)):

        @pl.when(step == near)
        def _():
            for other in range(RING):
                out[other] = results[other][:SUB]

    @pl.when(step == 3)
    def _():
        for other in range(RING):
            a_far_up[other] = results[other][:HALF]
            a_far_down[other] = results[other][HALF:SUB]

    b_own[0] = results[0][SUB:]
    b_up[0] = results[1][SUB:]
    b_down[0] = results[2][SUB:]
    b_far_up[0] = results[3][SUB : SUB + HALF]
    b_far_down[0] = results[3][SUB + HALF :]


def contributions(place, spec, tables, tables_t):
    facets = tables.shape[0]
    cols, rows = spec.shape[2:]
    flops = facets * 2 * 2 * 512 * 512 * 256
    full = jax.ShapeDtypeStruct((RING, SUB, SUB), jnp.bfloat16)
    part = jax.ShapeDtypeStruct((RING, HALF, SUB), jnp.bfloat16)
    shapes = (full, full, full, part, part)
    whole = tuple(pl.BlockSpec(s.shape, lambda t, place: (0, 0, 0)) for s in shapes)
    stepped = tuple(pl.BlockSpec((1,) + s.shape[1:], lambda t, place: (t, 0, 0)) for s in shapes)
    return pl.pallas_call(
        contribution_kernel,
        out_shape=shapes + shapes,
        grid_spec=pltpu.PrefetchScalarGridSpec(
            num_scalar_prefetch=1,
            grid=(RING,),
            in_specs=[
                pl.BlockSpec((1, 2, cols, rows), lambda t, place: (0, 0, 0, 0)),
                pl.BlockSpec((1, 2, MC, SUB), lambda t, place: (place[0], 0, 0, 0)),
                pl.BlockSpec((1, 2, SUB, MC), lambda t, place: (place[1], 0, 0, 0)),
            ],
            out_specs=whole + stepped,
            scratch_shapes=[
                pltpu.VMEM((2, 2, cols, rows - STEP), jnp.bfloat16),
                pltpu.VMEM((2 * MC, 2 * SUB), jnp.bfloat16),
                pltpu.VMEM((2 * SUB, 2 * MC), jnp.bfloat16),
            ],
        ),
        compiler_params=pltpu.CompilerParams(vmem_limit_bytes=VMEM_LIMIT),
        cost_estimate=pl.CostEstimate(flops=flops, bytes_accessed=8 * MIB, transcendentals=0),
        name="facet_contributions",
    )(place, spec, tables_t, tables)


def weights_kernel(offsets, fractions, u_out, v_out):
    cells = lax.broadcasted_iota(jnp.int32, (SUB, BLOCK), 0).astype(jnp.float32)
    scale = -((9.0 / KS) ** 2) / math.log(2.0)
    for axis, out in enumerate((u_out, v_out)):
        first = offsets[0, axis : axis + 1, :].astype(jnp.float32)
        inside = jnp.abs(cells - (first + 0.5 * (KS - 1))) < 0.5 * KS
        distance = cells - (first + (fractions[0, axis : axis + 1, :] + (0.5 * KS - 1.0)))
        weights = jnp.exp2(distance * distance * scale - 1.0)
        out[...] = jnp.where(inside, weights, 0.0).astype(jnp.bfloat16)


def kernel_weights(offsets, fractions):
    slots = offsets.shape[2]
    block_in = pl.BlockSpec((1, 2, BLOCK), lambda b: (0, 0, b))
    block_out = pl.BlockSpec((SUB, BLOCK), lambda b: (0, b))
    shape = jax.ShapeDtypeStruct((SUB, slots), jnp.bfloat16)
    return pl.pallas_call(
        weights_kernel,
        out_shape=(shape, shape),
        grid=(slots // BLOCK,),
        in_specs=[block_in, block_in],
        out_specs=(block_out, block_out),
        compiler_params=pltpu.CompilerParams(vmem_limit_bytes=VMEM_LIMIT),
        cost_estimate=pl.CostEstimate(
            flops=20 * SUB * slots, bytes_accessed=4 * SUB * slots, transcendentals=2 * SUB * slots
        ),
        name="kernel_weights",
    )(offsets, fractions)


def residual_kernel(count, *refs):
    grid_parts = refs[:6]
    u_in, v_in, observed, resid_out, re_out, im_out, grid, total = refs[6:]
    step = pl.program_id(0)

    @pl.when(step == 0)
    def _():
        total[...] = jnp.zeros_like(total)
        for part in range(2):
            own, low, high = (ref[0].astype(jnp.float32) for ref in grid_parts[3 * part : 3 * part + 3])
            grid[part * SUB : (part + 1) * SUB] = (own + low + high).astype(jnp.bfloat16)

    u_half = u_in[...]
    v_wide = v_in[...].astype(jnp.float32)
    product = f32_dot(grid[...], u_half)
    slot = step * BLOCK + lax.broadcasted_iota(jnp.int32, (1, BLOCK), 1)
    live = slot < count[0]
    for part in range(2):
        model = jnp.sum(product[part * SUB : (part + 1) * SUB] * v_wide, axis=0, keepdims=True)
        resid = jnp.where(live, observed[0, part : part + 1, :] - model, 0.0)
        resid_out[0, part : part + 1, :] = resid
        weighted = (resid * v_wide).astype(jnp.bfloat16)
        total[part * SUB : (part + 1) * SUB] += lax.dot_general(
            u_half, weighted, (((1,), (1,)), ((), ())), preferred_element_type=jnp.float32
        )

    @pl.when(step == pl.num_programs(0) - 1)
    def _():
        re_out[0] = total[:SUB].astype(jnp.bfloat16)
        im_out[0] = total[SUB:].astype(jnp.bfloat16)


def residuals(count, grid_parts, u_weights, v_weights, observed):
    slots = observed.shape[2]
    vis_block = pl.BlockSpec((1, 2, BLOCK), lambda b, count: (0, 0, b))
    weight_block = pl.BlockSpec((SUB, BLOCK), lambda b, count: (0, b))
    whole = pl.BlockSpec((1, SUB, SUB), lambda b, count: (0, 0, 0))
    half = jax.ShapeDtypeStruct((1, SUB, SUB), jnp.bfloat16)
    return pl.pallas_call(
        residual_kernel,
        out_shape=(jax.ShapeDtypeStruct(observed.shape, jnp.float32), half, half),
        grid_spec=pltpu.PrefetchScalarGridSpec(
            num_scalar_prefetch=1,
            grid=(slots // BLOCK,),
            in_specs=[whole] * 6 + [weight_block, weight_block, vis_block],
            out_specs=(vis_block, whole, whole),
            scratch_shapes=[
                pltpu.VMEM((2 * SUB, SUB), jnp.bfloat16),
                pltpu.VMEM((2 * SUB, SUB), jnp.float32),
            ],
        ),
        compiler_params=pltpu.CompilerParams(vmem_limit_bytes=VMEM_LIMIT),
        cost_estimate=pl.CostEstimate(
            flops=4 * 512 * 256 * slots, bytes_accessed=4 * SUB * slots, transcendentals=0
        ),
        name="residuals",
    )(count, *grid_parts, u_weights, v_weights, observed)


def adjoint_kernel(place, *refs):
    re_own, re_high, re_low, re_far_low, re_far_high = refs[:5]
    im_own, im_high, im_low, im_far_low, im_far_high = refs[5:10]
    left, right, kept, given, plane, im_all, left_mat, right_mat = refs[10:]
    step = pl.program_id(0)
    band_rows, cols = kept.shape[2:]

    @pl.when(step == 0)
    def _():
        plane[...] = jnp.zeros_like(plane)
        im_all[0] = im_own[...]
        im_all[1] = im_high[...]
        im_all[2] = im_low[...]
        im_all[3, :, :HALF] = im_far_low[...]
        im_all[3, :, HALF:] = im_far_high[...]
        a_re, a_im = left[0, 0], left[0, 1]
        left_mat[...] = stacked(side_by_side(a_re, a_im), side_by_side(-a_im, a_re))
        b_re, b_im = right[0, 0], right[0, 1]
        right_mat[...] = stacked(side_by_side(b_re, -b_im), side_by_side(b_im, b_re))

    re_blocks = (re_own[0], re_high[0], re_low[0], stacked(re_far_low[0], re_far_high[0]))
    edge = jnp.zeros((MC, LANES), jnp.float32)
    for other in range(RING):
        source = step * RING + other
        top = pl.multiple_of(place[2 + 2 * source] * STEP, STEP)
        left_col = place[3 + 2 * source]
        odd = left_col // STEP % 2
        col = pl.multiple_of(left_col // LANES * LANES, LANES)
        grid = stacked(re_blocks[other], im_all[step, other])
        half = f32_dot(left_mat[...], grid).astype(jnp.bfloat16)
        whole = f32_dot(side_by_side(half[:MC], half[MC:]), right_mat[...])
        for part in range(2):
            wide = side_by_side(whole[:, part * MC : (part + 1) * MC], edge)
            plane[part, pl.ds(top, MC), pl.ds(col, MC + LANES)] += pltpu.roll(wide, odd * STEP, 1)

    @pl.when(step == RING - 1)
    def _():
        for group, out in enumerate((kept, given)):
            for near in range(RING):
                band = place[2 + 2 * RING * RING + RING * group + near]
                first = pl.multiple_of(band * band_rows, 8)
                for part in range(2):
                    rows = plane[part, pl.ds(first, band_rows), :]
                    out[near, part] = rows[:, :cols].astype(jnp.bfloat16)


def adjoint_plane(place, re_parts, im_parts, tables, tables_t, bands, rows, cols):
    facets = tables.shape[0]
    flops = facets * 2 * 2 * 512 * 512 * 256
    wide = (cols + LANES - 1) // LANES * LANES
    band_shape = (RING, 2, rows // bands, cols)
    stepped = [pl.BlockSpec((1,) + x.shape[1:], lambda t, place: (t, 0, 0)) for x in re_parts]
    whole = [pl.BlockSpec(x.shape, lambda t, place: (0, 0, 0)) for x in im_parts]
    return pl.pallas_call(
        adjoint_kernel,
        out_shape=(jax.ShapeDtypeStruct(band_shape, jnp.bfloat16),) * 2,
        grid_spec=pltpu.PrefetchScalarGridSpec(
            num_scalar_prefetch=1,
            grid=(RING,),
            in_specs=stepped
            + whole
            + [
                pl.BlockSpec((1, 2, MC, SUB), lambda t, place: (place[0], 0, 0, 0)),
                pl.BlockSpec((1, 2, SUB, MC), lambda t, place: (place[1], 0, 0, 0)),
            ],
            out_specs=(pl.BlockSpec(band_shape, lambda t, place: (0, 0, 0, 0)),) * 2,
            scratch_shapes=[
                pltpu.VMEM((2, rows, wide), jnp.float32),
                pltpu.VMEM((RING, RING, SUB, SUB), jnp.bfloat16),
                pltpu.VMEM((2 * MC, 2 * SUB), jnp.bfloat16),
                pltpu.VMEM((2 * SUB, 2 * MC), jnp.bfloat16),
            ],
        ),
        compiler_params=pltpu.CompilerParams(vmem_limit_bytes=VMEM_LIMIT),
        cost_estimate=pl.CostEstimate(flops=flops, bytes_accessed=8 * MIB, transcendentals=0),
        name="adjoint_plane",
    )(place, *re_parts, *im_parts, tables_t, tables)


def along_x(shift):
    return "facet", [(i, (i // RING + shift) % RING * RING + i % RING) for i in range(RING * RING)]


def along_y(shift):
    return "facet", [(i, i // RING * RING + (i % RING + shift) % RING) for i in range(RING * RING)]


def along_z(shift):
    return "sub", [(i, (i // 2 + shift) % RING * 2 + i % 2) for i in range(2 * RING)]


def move(value, route):
    return lax.ppermute(value, *route)


def places(worker):
    facet = lax.axis_index("facet")
    sub = lax.axis_index("sub")
    subs = lax.axis_size("sub")
    near = jnp.asarray(NEAR, jnp.int32)
    x_near = (facet // RING + near) % RING
    y_near = (facet % RING + near) % RING
    rows = (x_near[:, None] * RING + y_near[None, :]).reshape(-1) * subs + sub
    ids = jnp.arange(worker.shape[0], dtype=jnp.int32)
    held = jnp.sum(jnp.where(worker[None, :] == rows[:, None], ids[None, :], 0), axis=1)
    head = jnp.stack([facet, jnp.mod(5 * facet + 3, RING * RING)]).astype(jnp.int32)
    corners = jnp.stack([held // subs, held % subs * STEP], axis=1).reshape(-1)
    z_near = (sub // 2 + near) % RING * 2
    bands = jnp.concatenate([z_near + sub % 2, z_near + 1 - sub % 2])
    return jnp.concatenate([head, corners, bands]).astype(jnp.int32)


def add_rows(block, first, second):
    upper, lower = block[:, :HALF], block[:, HALF:]
    if first is not None:
        upper = upper + first
    if second is not None:
        lower = lower + second
    return jnp.concatenate([upper, lower], axis=1)


def reduce_rings(pieces, routes):
    firsts = []
    for (_, _, _, far_up, far_down), route in zip(pieces, routes):
        firsts.append((move(far_up, route(1)), move(far_down, route(-1))))
    firsts = lax.optimization_barrier(firsts)
    seconds = []
    for (_, up, down, _, _), route, (low, high) in zip(pieces, routes, firsts):
        seconds.append((add_rows(up, low, None), add_rows(down, None, high)))
    arrived = [(move(up, route(1)), move(down, route(-1))) for (up, down), route in zip(seconds, routes)]
    arrived = lax.optimization_barrier(arrived)
    return [(piece[0],) + pair for piece, pair in zip(pieces, arrived)]


def gather_rings(blocks, routes):
    near = [(move(block, route(-1)), move(block, route(1))) for block, route in zip(blocks, routes)]
    near = lax.optimization_barrier(near)
    far = [
        (move(low[:, :HALF], route(1)), move(high[:, HALF:], route(-1)))
        for (high, low), route in zip(near, routes)
    ]
    far = lax.optimization_barrier(far)
    return [(block,) + pair + ends for block, pair, ends in zip(blocks, near, far)]


def in_one(parts):
    own, high, low, far_low, far_high = parts
    return jnp.concatenate([own, high, low, jnp.concatenate([far_low, far_high], axis=1)], axis=0)


def sum_rings(kept, given):
    swapped = lax.ppermute(given, "sub", [(i, i ^ 1) for i in range(2 * RING)])
    far = (kept[3] + swapped[3])
    low = move(far[0], along_z(1))
    high = move(far[1], along_z(-1))
    low, high = lax.optimization_barrier((low, high))
    up = jnp.stack([kept[1, 0] + swapped[1, 0] + low, kept[1, 1] + swapped[1, 1]])
    down = jnp.stack([kept[2, 0] + swapped[2, 0], kept[2, 1] + swapped[2, 1] + high])
    low, high = move(up, along_z(1)), move(down, along_z(-1))
    wide = [x.astype(jnp.float32) for x in (kept[0], swapped[0], low, high)]
    return wide[0] + wide[1] + wide[2] + wide[3]


def on_device(facet_spec, worker_of_subgrid, vis_count, bin_offsets, bin_fractions, observed):
    subs = lax.axis_size("sub")
    rows, cols = facet_spec.shape[2:]
    table = phase_tables(lax.axis_size("facet"))
    tables = jnp.asarray(table)
    tables_t = jnp.asarray(np.ascontiguousarray(table.transpose(0, 1, 3, 2)))
    routes = (along_x, along_y)
    place = places(worker_of_subgrid)
    outs = contributions(place, jnp.swapaxes(facet_spec, 2, 3), tables, tables_t)
    u_weights, v_weights = kernel_weights(bin_offsets, bin_fractions)
    sums = reduce_rings((outs[:5], outs[5:]), routes)
    again = []
    for own, low, high in sums:
        total = own.astype(jnp.float32) + low.astype(jnp.float32) + high.astype(jnp.float32)
        total = total.astype(jnp.bfloat16)
        again.append(
            (total[:1], total[1:2], total[2:3], total[3:4, :HALF], total[3:4, HALF:])
        )
    sums = reduce_rings(again, routes[::-1])
    residual, re_part, im_part = residuals(
        vis_count, sums[0] + sums[1], u_weights, v_weights, observed
    )
    gathered = gather_rings((re_part, im_part), routes)
    gathered = gather_rings([in_one(parts) for parts in gathered], routes[::-1])
    kept, given = adjoint_plane(
        place, gathered[0], gathered[1], tables, tables_t, subs, rows, cols
    )
    update = sum_rings(kept, given)
    return (residual, update[None])


def solution(mesh):
    placed = (
        P("facet", None, None, None),
        P(),
        P(("facet", "sub")),
        P(("facet", "sub"), None, None),
        P(("facet", "sub"), None, None),
        P(("facet", "sub"), None, None),
    )
    return jax.shard_map(
        on_device,
        mesh=mesh,
        in_specs=placed,
        out_specs=(P(("facet", "sub"), None, None), P("facet", None, "sub", None)),
        check_vma=False,
    )
```

```python
import math

import jax
import jax.numpy as jnp
import numpy as np
from jax import lax
from jax.experimental import pallas as pl
from jax.experimental.pallas import tpu as pltpu
from jax.sharding import PartitionSpec as P

SUB = 256
MC = 256
STEP = 64
KS = 8
BLOCK = 2048
LANES = 128
HALF = SUB // 2
RING = 4
NEAR = (0, 1, RING - 1, 2)
MIB = 1 << 20
VMEM_LIMIT = 58 * MIB
SMALL_LIMIT = 30 * MIB


def phase_tables(facets):
    sub_part = (np.arange(SUB) - SUB // 2)[:, None]
    win_part = (np.arange(MC) - MC // 2)[None, :]
    modulus = SUB * facets
    tables = []
    for offset in range(facets):
        residue = np.mod(sub_part * win_part * facets + sub_part * offset, modulus)
        angles = residue.astype(np.float32).astype(np.float64) * (2.0 * math.pi / modulus)
        factor = MC ** (-0.5)
        tables.append(np.stack([np.cos(angles) * factor, np.sin(angles) * factor]))
    return np.stack(tables).astype(jnp.bfloat16)


def side_by_side(*blocks):
    return jnp.concatenate(blocks, axis=1)


def stacked(*blocks):
    return jnp.concatenate(blocks, axis=0)


def f32_dot(left, right):
    return jnp.dot(left, right, preferred_element_type=jnp.float32)


def contribution_kernel(place, spec, left, right, *rest):
    a_own, a_up, a_down, a_far_up, a_far_down = rest[:5]
    b_own, b_up, b_down, b_far_up, b_far_down = rest[5:10]
    windows, left_mat, right_mat = rest[10:]
    step = pl.program_id(0)
    reach = windows.shape[3]

    @pl.when(step == 0)
    def _():
        for part in range(2):
            windows[0, part] = spec[0, part, :, :reach]
            windows[1, part] = spec[0, part, :, STEP : STEP + reach]
        a_re, a_im = left[0, 0], left[0, 1]
        right_mat[...] = stacked(side_by_side(a_re, a_im), side_by_side(-a_im, a_re))
        b_re, b_im = right[0, 0], right[0, 1]
        left_mat[...] = stacked(side_by_side(b_re, -b_im), side_by_side(b_im, b_re))

    views = []
    for other in range(RING):
        target = step * RING + other
        row_step = place[2 + 2 * target]
        first_col = pl.multiple_of(place[3 + 2 * target], STEP)
        odd = row_step % 2
        first_row = pl.multiple_of(row_step // 2 * LANES, LANES)
        views.append(
            side_by_side(
                windows[odd, 0, pl.ds(first_col, MC), pl.ds(first_row, MC)],
                windows[odd, 1, pl.ds(first_col, MC), pl.ds(first_row, MC)],
            )
        )
    halves = f32_dot(stacked(*views), right_mat[...]).astype(jnp.bfloat16)
    results = []
    for other in range(RING):
        half = halves[other * MC : (other + 1) * MC]
        whole = f32_dot(left_mat[...], stacked(half[:, :SUB], half[:, SUB:]))
        results.append(whole.astype(jnp.bfloat16))

    for near, out in ((0, a_own), (1, a_up), (2, a_down)):

        @pl.when(step == near)
        def _():
            for other in range(RING):
                out[other] = results[other][:SUB]

    @pl.when(step == 3)
    def _():
        for other in range(RING):
            a_far_up[other] = results[other][:HALF]
            a_far_down[other] = results[other][HALF:SUB]

    b_own[0] = results[0][SUB:]
    b_up[0] = results[1][SUB:]
    b_down[0] = results[2][SUB:]
    b_far_up[0] = results[3][SUB : SUB + HALF]
    b_far_down[0] = results[3][SUB + HALF :]


def contributions(place, spec, tables, tables_t):
    facets = tables.shape[0]
    cols, rows = spec.shape[2:]
    flops = facets * 2 * 2 * 512 * 512 * 256
    full = jax.ShapeDtypeStruct((RING, SUB, SUB), jnp.bfloat16)
    part = jax.ShapeDtypeStruct((RING, HALF, SUB), jnp.bfloat16)
    shapes = (full, full, full, part, part)
    whole = tuple(pl.BlockSpec(s.shape, lambda t, place: (0, 0, 0)) for s in shapes)
    stepped = tuple(pl.BlockSpec((1,) + s.shape[1:], lambda t, place: (t, 0, 0)) for s in shapes)
    return pl.pallas_call(
        contribution_kernel,
        out_shape=shapes + shapes,
        grid_spec=pltpu.PrefetchScalarGridSpec(
            num_scalar_prefetch=1,
            grid=(RING,),
            in_specs=[
                pl.BlockSpec((1, 2, cols, rows), lambda t, place: (0, 0, 0, 0)),
                pl.BlockSpec((1, 2, MC, SUB), lambda t, place: (place[0], 0, 0, 0)),
                pl.BlockSpec((1, 2, SUB, MC), lambda t, place: (place[1], 0, 0, 0)),
            ],
            out_specs=whole + stepped,
            scratch_shapes=[
                pltpu.VMEM((2, 2, cols, rows - STEP), jnp.bfloat16),
                pltpu.VMEM((2 * MC, 2 * SUB), jnp.bfloat16),
                pltpu.VMEM((2 * SUB, 2 * MC), jnp.bfloat16),
            ],
        ),
        compiler_params=pltpu.CompilerParams(vmem_limit_bytes=VMEM_LIMIT),
        cost_estimate=pl.CostEstimate(flops=flops, bytes_accessed=8 * MIB, transcendentals=0),
        name="facet_contributions",
    )(place, spec, tables_t, tables)


def weights_kernel(offsets, fractions, u_out, v_out):
    cells = lax.broadcasted_iota(jnp.int32, (SUB, BLOCK), 0).astype(jnp.float32)
    scale = -((9.0 / KS) ** 2) / math.log(2.0)
    for axis, out in enumerate((u_out, v_out)):
        first = offsets[0, axis : axis + 1, :].astype(jnp.float32)
        inside = jnp.abs(cells - (first + 0.5 * (KS - 1))) < 0.5 * KS
        distance = cells - (first + (fractions[0, axis : axis + 1, :] + (0.5 * KS - 1.0)))
        weights = jnp.exp2(distance * distance * scale - 1.0)
        out[...] = jnp.where(inside, weights, 0.0).astype(jnp.bfloat16)


def kernel_weights(offsets, fractions):
    slots = offsets.shape[2]
    block_in = pl.BlockSpec((1, 2, BLOCK), lambda b: (0, 0, b))
    block_out = pl.BlockSpec((SUB, BLOCK), lambda b: (0, b))
    shape = jax.ShapeDtypeStruct((SUB, slots), jnp.bfloat16)
    return pl.pallas_call(
        weights_kernel,
        out_shape=(shape, shape),
        grid=(slots // BLOCK,),
        in_specs=[block_in, block_in],
        out_specs=(block_out, block_out),
        compiler_params=pltpu.CompilerParams(vmem_limit_bytes=SMALL_LIMIT),
        cost_estimate=pl.CostEstimate(
            flops=20 * SUB * slots, bytes_accessed=4 * SUB * slots, transcendentals=2 * SUB * slots
        ),
        name="kernel_weights",
    )(offsets, fractions)


def residual_kernel(count, *refs):
    grid_parts = refs[:8]
    u_in, v_in, observed, resid_out, re_out, im_out, grid, total = refs[8:]
    step = pl.program_id(0)

    @pl.when(step == 0)
    def _():
        total[...] = jnp.zeros_like(total)
        for part in range(2):
            own, *others = (ref[0].astype(jnp.float32) for ref in grid_parts[4 * part : 4 * part + 4])
            grid[part * SUB : (part + 1) * SUB] = sum(others, own).astype(jnp.bfloat16)

    u_half = u_in[...]
    v_wide = v_in[...].astype(jnp.float32)
    product = f32_dot(grid[...], u_half)
    slot = step * BLOCK + lax.broadcasted_iota(jnp.int32, (1, BLOCK), 1)
    live = slot < count[0]
    for part in range(2):
        model = jnp.sum(product[part * SUB : (part + 1) * SUB] * v_wide, axis=0, keepdims=True)
        resid = jnp.where(live, observed[0, part : part + 1, :] - model, 0.0)
        resid_out[0, part : part + 1, :] = resid
        weighted = (resid * v_wide).astype(jnp.bfloat16)
        total[part * SUB : (part + 1) * SUB] += lax.dot_general(
            u_half, weighted, (((1,), (1,)), ((), ())), preferred_element_type=jnp.float32
        )

    @pl.when(step == pl.num_programs(0) - 1)
    def _():
        re_out[0] = total[:SUB].astype(jnp.bfloat16)
        im_out[0] = total[SUB:].astype(jnp.bfloat16)


def residuals(count, grid_parts, u_weights, v_weights, observed):
    slots = observed.shape[2]
    vis_block = pl.BlockSpec((1, 2, BLOCK), lambda b, count: (0, 0, b))
    weight_block = pl.BlockSpec((SUB, BLOCK), lambda b, count: (0, b))
    whole = pl.BlockSpec((1, SUB, SUB), lambda b, count: (0, 0, 0))
    half = jax.ShapeDtypeStruct((1, SUB, SUB), jnp.bfloat16)
    return pl.pallas_call(
        residual_kernel,
        out_shape=(jax.ShapeDtypeStruct(observed.shape, jnp.float32), half, half),
        grid_spec=pltpu.PrefetchScalarGridSpec(
            num_scalar_prefetch=1,
            grid=(slots // BLOCK,),
            in_specs=[whole] * 8 + [weight_block, weight_block, vis_block],
            out_specs=(vis_block, whole, whole),
            scratch_shapes=[
                pltpu.VMEM((2 * SUB, SUB), jnp.bfloat16),
                pltpu.VMEM((2 * SUB, SUB), jnp.float32),
            ],
        ),
        compiler_params=pltpu.CompilerParams(vmem_limit_bytes=SMALL_LIMIT),
        cost_estimate=pl.CostEstimate(
            flops=4 * 512 * 256 * slots, bytes_accessed=4 * SUB * slots, transcendentals=0
        ),
        name="residuals",
    )(count, *grid_parts, u_weights, v_weights, observed)


def adjoint_kernel(place, *refs):
    re_own, re_high, re_low, re_far_low, re_far_high = refs[:5]
    im_own, im_high, im_low, im_far_low, im_far_high = refs[5:10]
    left, right, kept, given, plane, im_all, left_mat, right_mat = refs[10:]
    step = pl.program_id(0)
    band_rows, cols = kept.shape[2:]

    @pl.when(step == 0)
    def _():
        plane[...] = jnp.zeros_like(plane)
        im_all[0] = im_own[...]
        im_all[1] = im_high[...]
        im_all[2] = im_low[...]
        im_all[3, :, :HALF] = im_far_low[...]
        im_all[3, :, HALF:] = im_far_high[...]
        a_re, a_im = left[0, 0], left[0, 1]
        left_mat[...] = stacked(side_by_side(a_re, a_im), side_by_side(-a_im, a_re))
        b_re, b_im = right[0, 0], right[0, 1]
        right_mat[...] = stacked(side_by_side(b_re, -b_im), side_by_side(b_im, b_re))

    re_blocks = (re_own[0], re_high[0], re_low[0], stacked(re_far_low[0], re_far_high[0]))
    edge = jnp.zeros((MC, LANES), jnp.float32)
    halves = []
    for other in range(RING):
        grid = stacked(re_blocks[other], im_all[step, other])
        half = f32_dot(left_mat[...], grid).astype(jnp.bfloat16)
        halves.append(side_by_side(half[:MC], half[MC:]))
    wholes = f32_dot(stacked(*halves), right_mat[...])
    for other in range(RING):
        source = step * RING + other
        top = pl.multiple_of(place[2 + 2 * source] * STEP, STEP)
        left_col = place[3 + 2 * source]
        odd = left_col // STEP % 2
        col = pl.multiple_of(left_col // LANES * LANES, LANES)
        for part in range(2):
            whole = wholes[other * MC : (other + 1) * MC, part * MC : (part + 1) * MC]
            wide = pltpu.roll(side_by_side(whole, edge), odd * STEP, 1)
            plane[part, pl.ds(top, MC), pl.ds(col, MC + LANES)] += wide

    @pl.when(step == RING - 1)
    def _():
        for group, out in enumerate((kept, given)):
            for near in range(RING):
                band = place[2 + 2 * RING * RING + RING * group + near]
                first = pl.multiple_of(band * band_rows, 8)
                for part in range(2):
                    rows = plane[part, pl.ds(first, band_rows), :]
                    out[near, part] = rows[:, :cols].astype(jnp.bfloat16)


def adjoint_plane(place, re_parts, im_parts, tables, tables_t, bands, rows, cols):
    facets = tables.shape[0]
    flops = facets * 2 * 2 * 512 * 512 * 256
    wide = (cols + LANES - 1) // LANES * LANES
    band_shape = (RING, 2, rows // bands, cols)
    stepped = [pl.BlockSpec((1,) + x.shape[1:], lambda t, place: (t, 0, 0)) for x in re_parts]
    whole = [pl.BlockSpec(x.shape, lambda t, place: (0, 0, 0)) for x in im_parts]
    return pl.pallas_call(
        adjoint_kernel,
        out_shape=(jax.ShapeDtypeStruct(band_shape, jnp.bfloat16),) * 2,
        grid_spec=pltpu.PrefetchScalarGridSpec(
            num_scalar_prefetch=1,
            grid=(RING,),
            in_specs=stepped
            + whole
            + [
                pl.BlockSpec((1, 2, MC, SUB), lambda t, place: (place[0], 0, 0, 0)),
                pl.BlockSpec((1, 2, SUB, MC), lambda t, place: (place[1], 0, 0, 0)),
            ],
            out_specs=(pl.BlockSpec(band_shape, lambda t, place: (0, 0, 0, 0)),) * 2,
            scratch_shapes=[
                pltpu.VMEM((2, rows, wide), jnp.float32),
                pltpu.VMEM((RING, RING, SUB, SUB), jnp.bfloat16),
                pltpu.VMEM((2 * MC, 2 * SUB), jnp.bfloat16),
                pltpu.VMEM((2 * SUB, 2 * MC), jnp.bfloat16),
            ],
        ),
        compiler_params=pltpu.CompilerParams(vmem_limit_bytes=SMALL_LIMIT),
        cost_estimate=pl.CostEstimate(flops=flops, bytes_accessed=8 * MIB, transcendentals=0),
        name="adjoint_plane",
    )(place, *re_parts, *im_parts, tables_t, tables)


def along_x(shift):
    return "facet", [(i, (i // RING + shift) % RING * RING + i % RING) for i in range(RING * RING)]


def along_y(shift):
    return "facet", [(i, i // RING * RING + (i % RING + shift) % RING) for i in range(RING * RING)]


def along_z(shift):
    return "sub", [(i, (i // 2 + shift) % RING * 2 + i % 2) for i in range(2 * RING)]


def move(value, route):
    return lax.ppermute(value, *route)


def near_shift(index):
    return index ^ (index >> 1)


def places(worker):
    facet = lax.axis_index("facet")
    sub = lax.axis_index("sub")
    subs = lax.axis_size("sub")
    facets = RING * RING
    entry = jnp.arange(2 + 2 * facets + 2 * RING, dtype=jnp.int32)
    target = ((entry - 2) >> 1) & (facets - 1)
    x_at = ((facet >> 2) + near_shift(target >> 2)) & (RING - 1)
    y_at = (facet + near_shift(target & (RING - 1))) & (RING - 1)
    row = (x_at * RING + y_at) * subs + sub
    ids = jnp.arange(worker.shape[0], dtype=jnp.int32)
    held = jnp.sum(jnp.where(worker[None, :] == row[:, None], ids[None, :], 0), axis=1)
    corner = jnp.where(entry & 1 == 0, held >> 3, (held & (subs - 1)) * STEP)
    table = jnp.where(entry == 0, facet, (5 * facet + 3) & (facets - 1))
    band = entry - 2 - 2 * facets
    z_at = ((sub >> 1) + near_shift(band & (RING - 1))) & (RING - 1)
    band = z_at * 2 + ((sub & 1) ^ (band >> 2 & 1))
    return jnp.where(entry < 2, table, jnp.where(entry < 2 + 2 * facets, corner, band)).astype(jnp.int32)


def with_rows(block, rows, first):
    space = [(0, 0, 0)] * block.ndim
    space[-2] = (first, block.shape[-2] - rows.shape[-2] - first, 0)
    return block + lax.pad(rows, jnp.zeros((), rows.dtype), space)


def reduce_large(pieces, routes):
    sums = []
    for (own, up, down, far_up, far_down), route in zip(pieces, routes):
        low, high = move(far_up, route(1)), move(far_down, route(-1))
        up = with_rows(up, low, 0)
        down = with_rows(down, high, HALF)
        sums.append((own, move(up, route(1)), move(down, route(-1))))
    return sums


def reduce_small(blocks, routes):
    return [
        (block[:1],)
        + tuple(move(block[k : k + 1], route(NEAR[k])) for k in range(1, RING))
        for block, route in zip(blocks, routes)
    ]


def gather_rings(blocks, routes):
    parts = []
    for block, route in zip(blocks, routes):
        low, high = move(block, route(1)), move(block, route(-1))
        far = (move(low[:, :HALF], route(1)), move(high[:, HALF:], route(-1)))
        parts.append((block, high, low) + far)
    return parts


def in_one(parts):
    own, high, low, far_low, far_high = parts
    return jnp.concatenate([own, high, low, jnp.concatenate([far_low, far_high], axis=1)], axis=0)


def sum_rings(kept, given):
    swapped = lax.ppermute(given, "sub", [(i, i ^ 1) for i in range(2 * RING)])
    far = (kept[3] + swapped[3])
    low = move(far[0], along_z(1))
    high = move(far[1], along_z(-1))
    low, high = lax.optimization_barrier((low, high))
    nothing = jnp.zeros_like(low)
    up = kept[1] + swapped[1] + jnp.stack([low, nothing])
    down = kept[2] + swapped[2] + jnp.stack([nothing, high])
    low, high = move(up, along_z(1)), move(down, along_z(-1))
    wide = [x.astype(jnp.float32) for x in (kept[0], swapped[0], low, high)]
    return wide[0] + wide[1] + wide[2] + wide[3]


def on_device(facet_spec, worker_of_subgrid, vis_count, bin_offsets, bin_fractions, observed):
    subs = lax.axis_size("sub")
    rows, cols = facet_spec.shape[2:]
    table = phase_tables(lax.axis_size("facet"))
    tables = jnp.asarray(table)
    tables_t = jnp.asarray(np.ascontiguousarray(table.transpose(0, 1, 3, 2)))
    routes = (along_x, along_y)
    place = places(worker_of_subgrid)
    outs = contributions(place, jnp.swapaxes(facet_spec, 2, 3), tables, tables_t)
    first, bin_offsets = lax.optimization_barrier((outs[0], bin_offsets))
    weights = kernel_weights(bin_offsets, bin_fractions)
    first, weights = lax.optimization_barrier((first, weights))
    sums = reduce_large(((first,) + tuple(outs[1:5]), outs[5:]), routes)
    wide = [sum(x.astype(jnp.float32) for x in parts) for parts in sums]
    sums = reduce_small([x.astype(jnp.bfloat16) for x in wide], routes[::-1])
    residual, re_part, im_part = residuals(
        vis_count, sums[0] + sums[1], *weights, observed
    )
    gathered = gather_rings((re_part, im_part), routes)
    gathered = gather_rings([in_one(parts) for parts in gathered], routes[::-1])
    kept, given = adjoint_plane(
        place, gathered[0], gathered[1], tables, tables_t, subs, rows, cols
    )
    update = sum_rings(kept, given)
    return (residual, update[None])


def solution(mesh):
    placed = (
        P("facet", None, None, None),
        P(),
        P(("facet", "sub")),
        P(("facet", "sub"), None, None),
        P(("facet", "sub"), None, None),
        P(("facet", "sub"), None, None),
    )
    return jax.shard_map(
        on_device,
        mesh=mesh,
        in_specs=placed,
        out_specs=(P(("facet", "sub"), None, None), P("facet", None, "sub", None)),
        check_vma=False,
    )
```

```python
import math

import jax
import jax.numpy as jnp
import numpy as np
from jax import lax
from jax.experimental import pallas as pl
from jax.experimental.pallas import tpu as pltpu
from jax.sharding import PartitionSpec as P

SUB = 256
MC = 256
STEP = 64
KS = 8
BLOCK = 2048
LANES = 128
HALF = SUB // 2
RING = 4
NEAR = (0, 1, RING - 1, 2)
MIB = 1 << 20
FAR_LIMIT = 58 * MIB
NEAR_LIMIT = 36 * MIB
SMALL_LIMIT = 30 * MIB


def phase_parts(facets):
    sub_part = np.arange(SUB) - SUB // 2
    win_part = np.arange(MC) - MC // 2
    modulus = SUB * facets
    turns = 2.0 * math.pi / modulus
    residue = np.mod(win_part[:, None] * sub_part[None, :] * facets, modulus) * turns
    base = np.stack([np.cos(residue), np.sin(residue)]) * MC ** (-0.5)
    shift = np.mod(np.arange(facets)[:, None] * sub_part[None, :], modulus) * turns
    phases = np.stack([np.cos(shift), np.sin(shift)], axis=1)
    return base.astype(np.float32), phases.astype(np.float32)


def transposed_table(base, phase):
    turn_re, turn_im = phase[0, 0:1, :], phase[0, 1:2, :]
    re = base[0] * turn_re - base[1] * turn_im
    im = base[0] * turn_im + base[1] * turn_re
    return re, im


def side_by_side(*blocks):
    return jnp.concatenate(blocks, axis=1)


def stacked(*blocks):
    return jnp.concatenate(blocks, axis=0)


def f32_dot(left, right):
    return jnp.dot(left, right, preferred_element_type=jnp.float32)


def transformed(targets, place, spec, base, left, right, windows, left_mat, right_mat):
    reach = windows.shape[3]
    for part in range(2):
        windows[0, part] = spec[0, part, :, :reach]
        windows[1, part] = spec[0, part, :, STEP : STEP + reach]
    a_re, a_im = (x.astype(jnp.bfloat16) for x in transposed_table(base, left))
    right_mat[...] = stacked(side_by_side(a_re, a_im), side_by_side(-a_im, a_re))
    b_re, b_im = (x.T.astype(jnp.bfloat16) for x in transposed_table(base, right))
    left_mat[...] = stacked(side_by_side(b_re, -b_im), side_by_side(b_im, b_re))
    views = []
    for across, along in targets:
        target = across * RING + along
        row_step = place[2 + 2 * target]
        first_col = pl.multiple_of(place[3 + 2 * target], STEP)
        odd = row_step % 2
        first_row = pl.multiple_of(row_step // 2 * LANES, LANES)
        views.append(
            side_by_side(
                windows[odd, 0, pl.ds(first_col, MC), pl.ds(first_row, MC)],
                windows[odd, 1, pl.ds(first_col, MC), pl.ds(first_row, MC)],
            )
        )
    halves = f32_dot(stacked(*views), right_mat[...]).astype(jnp.bfloat16)
    results = {}
    for count, target in enumerate(targets):
        half = halves[count * MC : (count + 1) * MC]
        whole = f32_dot(left_mat[...], stacked(half[:, :SUB], half[:, SUB:]))
        results[target] = whole.astype(jnp.bfloat16)
    return results


FAR = RING - 1
FAR_TARGETS = tuple((FAR, k) for k in range(RING)) + tuple((k, FAR) for k in range(FAR))
NEAR_TARGETS = tuple((i, k) for i in range(FAR) for k in range(FAR))


def far_kernel(place, spec, base, left, right, *rest):
    a_far_up, a_far_down, b_far_up, b_far_down, a_last, b_last = rest[:6]
    results = transformed(FAR_TARGETS, place, spec, base, left, right, *rest[6:])
    for k in range(RING):
        a_far_up[k] = results[FAR, k][:HALF]
        a_far_down[k] = results[FAR, k][HALF:SUB]
        b_far_up[k] = results[k, FAR][SUB : SUB + HALF]
        b_far_down[k] = results[k, FAR][SUB + HALF :]
    for k in range(FAR):
        a_last[k] = results[k, FAR][:SUB]
        b_last[k] = results[FAR, k][SUB:]


def near_kernel(place, spec, base, left, right, a_last, b_last, *rest):
    a_outs, b_outs = rest[:3], rest[3:6]
    results = transformed(NEAR_TARGETS, place, spec, base, left, right, *rest[6:])
    for i in range(FAR):
        for k in range(FAR):
            a_outs[i][k] = results[i, k][:SUB]
            b_outs[k][i] = results[i, k][SUB:]
        a_outs[i][FAR] = a_last[i]
        b_outs[i][FAR] = b_last[i]


def contributions(kernel, name, limit, shapes, place, spec, base, phases, lasts=()):
    cols, rows = spec.shape[2:]
    whole = [pl.BlockSpec(x.shape, lambda t, place: (0, 0, 0)) for x in lasts]
    return pl.pallas_call(
        kernel,
        out_shape=tuple(jax.ShapeDtypeStruct(s, jnp.bfloat16) for s in shapes),
        grid_spec=pltpu.PrefetchScalarGridSpec(
            num_scalar_prefetch=1,
            grid=(1,),
            in_specs=[
                pl.BlockSpec((1, 2, cols, rows), lambda t, place: (0, 0, 0, 0)),
                pl.BlockSpec((2, MC, SUB), lambda t, place: (0, 0, 0)),
                pl.BlockSpec((1, 2, SUB), lambda t, place: (place[0], 0, 0)),
                pl.BlockSpec((1, 2, SUB), lambda t, place: (place[1], 0, 0)),
            ]
            + whole,
            out_specs=tuple(pl.BlockSpec(s, lambda t, place: (0, 0, 0)) for s in shapes),
            scratch_shapes=[
                pltpu.VMEM((2, 2, cols, rows - STEP), jnp.bfloat16),
                pltpu.VMEM((2 * SUB, 2 * MC), jnp.bfloat16),
                pltpu.VMEM((2 * MC, 2 * SUB), jnp.bfloat16),
            ],
        ),
        compiler_params=pltpu.CompilerParams(vmem_limit_bytes=limit),
        cost_estimate=pl.CostEstimate(
            flops=8 * 2 * 2 * 512 * 512 * 256, bytes_accessed=8 * MIB, transcendentals=0
        ),
        name=name,
    )(place, spec, base, phases, phases, *lasts)


def weights_kernel(offsets, fractions, u_out, v_out):
    cells = lax.broadcasted_iota(jnp.int32, (SUB, BLOCK), 0).astype(jnp.float32)
    scale = -((9.0 / KS) ** 2) / math.log(2.0)
    for axis, out in enumerate((u_out, v_out)):
        first = offsets[0, axis : axis + 1, :].astype(jnp.float32)
        inside = jnp.abs(cells - (first + 0.5 * (KS - 1))) < 0.5 * KS
        distance = cells - (first + (fractions[0, axis : axis + 1, :] + (0.5 * KS - 1.0)))
        weights = jnp.exp2(distance * distance * scale - 1.0)
        out[...] = jnp.where(inside, weights, 0.0).astype(jnp.bfloat16)


def kernel_weights(offsets, fractions):
    slots = offsets.shape[2]
    block_in = pl.BlockSpec((1, 2, BLOCK), lambda b: (0, 0, b))
    block_out = pl.BlockSpec((SUB, BLOCK), lambda b: (0, b))
    shape = jax.ShapeDtypeStruct((SUB, slots), jnp.bfloat16)
    return pl.pallas_call(
        weights_kernel,
        out_shape=(shape, shape),
        grid=(slots // BLOCK,),
        in_specs=[block_in, block_in],
        out_specs=(block_out, block_out),
        compiler_params=pltpu.CompilerParams(vmem_limit_bytes=SMALL_LIMIT),
        cost_estimate=pl.CostEstimate(
            flops=20 * SUB * slots, bytes_accessed=4 * SUB * slots, transcendentals=2 * SUB * slots
        ),
        name="kernel_weights",
    )(offsets, fractions)


def residual_kernel(count, *refs):
    grid_parts = refs[:8]
    u_in, v_in, observed, resid_out, re_out, im_out, grid, total = refs[8:]
    step = pl.program_id(0)

    @pl.when(step == 0)
    def _():
        total[...] = jnp.zeros_like(total)
        for part in range(2):
            own, *others = (ref[0].astype(jnp.float32) for ref in grid_parts[4 * part : 4 * part + 4])
            grid[part * SUB : (part + 1) * SUB] = sum(others, own).astype(jnp.bfloat16)

    u_half = u_in[...]
    v_wide = v_in[...].astype(jnp.float32)
    product = f32_dot(grid[...], u_half)
    slot = step * BLOCK + lax.broadcasted_iota(jnp.int32, (1, BLOCK), 1)
    live = slot < count[0]
    for part in range(2):
        model = jnp.sum(product[part * SUB : (part + 1) * SUB] * v_wide, axis=0, keepdims=True)
        resid = jnp.where(live, observed[0, part : part + 1, :] - model, 0.0)
        resid_out[0, part : part + 1, :] = resid
        weighted = (resid * v_wide).astype(jnp.bfloat16)
        total[part * SUB : (part + 1) * SUB] += lax.dot_general(
            u_half, weighted, (((1,), (1,)), ((), ())), preferred_element_type=jnp.float32
        )

    @pl.when(step == pl.num_programs(0) - 1)
    def _():
        re_out[0] = total[:SUB].astype(jnp.bfloat16)
        im_out[0] = total[SUB:].astype(jnp.bfloat16)


def residuals(count, grid_parts, u_weights, v_weights, observed):
    slots = observed.shape[2]
    vis_block = pl.BlockSpec((1, 2, BLOCK), lambda b, count: (0, 0, b))
    weight_block = pl.BlockSpec((SUB, BLOCK), lambda b, count: (0, b))
    whole = pl.BlockSpec((1, SUB, SUB), lambda b, count: (0, 0, 0))
    half = jax.ShapeDtypeStruct((1, SUB, SUB), jnp.bfloat16)
    return pl.pallas_call(
        residual_kernel,
        out_shape=(jax.ShapeDtypeStruct(observed.shape, jnp.float32), half, half),
        grid_spec=pltpu.PrefetchScalarGridSpec(
            num_scalar_prefetch=1,
            grid=(slots // BLOCK,),
            in_specs=[whole] * 8 + [weight_block, weight_block, vis_block],
            out_specs=(vis_block, whole, whole),
            scratch_shapes=[
                pltpu.VMEM((2 * SUB, SUB), jnp.bfloat16),
                pltpu.VMEM((2 * SUB, SUB), jnp.float32),
            ],
        ),
        compiler_params=pltpu.CompilerParams(vmem_limit_bytes=SMALL_LIMIT),
        cost_estimate=pl.CostEstimate(
            flops=4 * 512 * 256 * slots, bytes_accessed=4 * SUB * slots, transcendentals=0
        ),
        name="residuals",
    )(count, *grid_parts, u_weights, v_weights, observed)


def adjoint_kernel(place, *refs):
    re_own, re_high, re_low, re_far_low, re_far_high = refs[:5]
    im_own, im_high, im_low, im_far_low, im_far_high = refs[5:10]
    base, left, right, kept, given, plane, im_all, left_mat, right_mat = refs[10:]
    step = pl.program_id(0)
    band_rows, cols = kept.shape[2:]

    @pl.when(step == 0)
    def _():
        plane[...] = jnp.zeros_like(plane)
        im_all[0] = im_own[...]
        im_all[1] = im_high[...]
        im_all[2] = im_low[...]
        im_all[3, :, :HALF] = im_far_low[...]
        im_all[3, :, HALF:] = im_far_high[...]
        a_re, a_im = (x.astype(jnp.bfloat16) for x in transposed_table(base, left))
        left_mat[...] = stacked(side_by_side(a_re, a_im), side_by_side(-a_im, a_re))
        b_re, b_im = (x.T.astype(jnp.bfloat16) for x in transposed_table(base, right))
        right_mat[...] = stacked(side_by_side(b_re, -b_im), side_by_side(b_im, b_re))

    re_blocks = (re_own[0], re_high[0], re_low[0], stacked(re_far_low[0], re_far_high[0]))
    edge = jnp.zeros((MC, LANES), jnp.float32)
    halves = []
    for other in range(RING):
        grid = stacked(re_blocks[other], im_all[step, other])
        half = f32_dot(left_mat[...], grid).astype(jnp.bfloat16)
        halves.append(side_by_side(half[:MC], half[MC:]))
    wholes = f32_dot(stacked(*halves), right_mat[...])
    for other in range(RING):
        source = step * RING + other
        top = pl.multiple_of(place[2 + 2 * source] * STEP, STEP)
        left_col = place[3 + 2 * source]
        odd = left_col // STEP % 2
        col = pl.multiple_of(left_col // LANES * LANES, LANES)
        for part in range(2):
            whole = wholes[other * MC : (other + 1) * MC, part * MC : (part + 1) * MC]
            wide = pltpu.roll(side_by_side(whole, edge), odd * STEP, 1)
            plane[part, pl.ds(top, MC), pl.ds(col, MC + LANES)] += wide

    @pl.when(step == RING - 1)
    def _():
        for group, out in enumerate((kept, given)):
            for near in range(RING):
                band = place[2 + 2 * RING * RING + RING * group + near]
                first = pl.multiple_of(band * band_rows, 8)
                for part in range(2):
                    rows = plane[part, pl.ds(first, band_rows), :]
                    out[near, part] = rows[:, :cols].astype(jnp.bfloat16)


def adjoint_plane(place, re_parts, im_parts, base, phases, bands, rows, cols):
    facets = phases.shape[0]
    flops = facets * 2 * 2 * 512 * 512 * 256
    wide = (cols + LANES - 1) // LANES * LANES
    band_shape = (RING, 2, rows // bands, cols)
    stepped = [pl.BlockSpec((1,) + x.shape[1:], lambda t, place: (t, 0, 0)) for x in re_parts]
    whole = [pl.BlockSpec(x.shape, lambda t, place: (0, 0, 0)) for x in im_parts]
    return pl.pallas_call(
        adjoint_kernel,
        out_shape=(jax.ShapeDtypeStruct(band_shape, jnp.bfloat16),) * 2,
        grid_spec=pltpu.PrefetchScalarGridSpec(
            num_scalar_prefetch=1,
            grid=(RING,),
            in_specs=stepped
            + whole
            + [
                pl.BlockSpec((2, MC, SUB), lambda t, place: (0, 0, 0)),
                pl.BlockSpec((1, 2, SUB), lambda t, place: (place[0], 0, 0)),
                pl.BlockSpec((1, 2, SUB), lambda t, place: (place[1], 0, 0)),
            ],
            out_specs=(pl.BlockSpec(band_shape, lambda t, place: (0, 0, 0, 0)),) * 2,
            scratch_shapes=[
                pltpu.VMEM((2, rows, wide), jnp.float32),
                pltpu.VMEM((RING, RING, SUB, SUB), jnp.bfloat16),
                pltpu.VMEM((2 * MC, 2 * SUB), jnp.bfloat16),
                pltpu.VMEM((2 * SUB, 2 * MC), jnp.bfloat16),
            ],
        ),
        compiler_params=pltpu.CompilerParams(vmem_limit_bytes=SMALL_LIMIT),
        cost_estimate=pl.CostEstimate(flops=flops, bytes_accessed=8 * MIB, transcendentals=0),
        name="adjoint_plane",
    )(place, *re_parts, *im_parts, base, phases, phases)


def along_x(shift):
    return "facet", [(i, (i // RING + shift) % RING * RING + i % RING) for i in range(RING * RING)]


def along_y(shift):
    return "facet", [(i, i // RING * RING + (i % RING + shift) % RING) for i in range(RING * RING)]


def along_z(shift):
    return "sub", [(i, (i // 2 + shift) % RING * 2 + i % 2) for i in range(2 * RING)]


def move(value, route):
    return lax.ppermute(value, *route)


def near_shift(index):
    return index ^ (index >> 1)


def places(worker):
    facet = lax.axis_index("facet")
    sub = lax.axis_index("sub")
    subs = lax.axis_size("sub")
    facets = RING * RING
    entry = jnp.arange(2 + 2 * facets + 2 * RING, dtype=jnp.int32)
    target = ((entry - 2) >> 1) & (facets - 1)
    x_at = ((facet >> 2) + near_shift(target >> 2)) & (RING - 1)
    y_at = (facet + near_shift(target & (RING - 1))) & (RING - 1)
    row = (x_at * RING + y_at) * subs + sub
    ids = jnp.arange(worker.shape[0], dtype=jnp.int32)
    held = jnp.sum(jnp.where(worker[None, :] == row[:, None], ids[None, :], 0), axis=1)
    corner = jnp.where(entry & 1 == 0, held >> 3, (held & (subs - 1)) * STEP)
    table = jnp.where(entry == 0, facet, (5 * facet + 3) & (facets - 1))
    band = entry - 2 - 2 * facets
    z_at = ((sub >> 1) + near_shift(band & (RING - 1))) & (RING - 1)
    band = z_at * 2 + ((sub & 1) ^ (band >> 2 & 1))
    return jnp.where(entry < 2, table, jnp.where(entry < 2 + 2 * facets, corner, band)).astype(jnp.int32)


def with_rows(block, rows, first):
    space = [(0, 0, 0)] * block.ndim
    space[-2] = (first, block.shape[-2] - rows.shape[-2] - first, 0)
    return block + lax.pad(rows, jnp.zeros((), rows.dtype), space)


def send_far(far_up, far_down, route):
    return move(far_up, route(1)), move(far_down, route(-1))


def send_near(up, down, arrived, route):
    low, high = arrived
    return move(with_rows(up, low, 0), route(1)), move(with_rows(down, high, HALF), route(-1))


def reduce_small(blocks, routes):
    return [
        (block[:1],)
        + tuple(move(block[k : k + 1], route(NEAR[k])) for k in range(1, RING))
        for block, route in zip(blocks, routes)
    ]


def gather_rings(blocks, routes):
    parts = []
    for block, route in zip(blocks, routes):
        low, high = move(block, route(1)), move(block, route(-1))
        far = (move(low[:, :HALF], route(1)), move(high[:, HALF:], route(-1)))
        parts.append((block, high, low) + far)
    return parts


def in_one(parts):
    own, high, low, far_low, far_high = parts
    return jnp.concatenate([own, high, low, jnp.concatenate([far_low, far_high], axis=1)], axis=0)


def sum_rings(kept, given):
    swapped = lax.ppermute(given, "sub", [(i, i ^ 1) for i in range(2 * RING)])
    far = (kept[3] + swapped[3])
    low = move(far[0], along_z(1))
    high = move(far[1], along_z(-1))
    low, high = lax.optimization_barrier((low, high))
    nothing = jnp.zeros_like(low)
    up = kept[1] + swapped[1] + jnp.stack([low, nothing])
    down = kept[2] + swapped[2] + jnp.stack([nothing, high])
    low, high = move(up, along_z(1)), move(down, along_z(-1))
    wide = [x.astype(jnp.float32) for x in (kept[0], swapped[0], low, high)]
    return wide[0] + wide[1] + wide[2] + wide[3]


def on_device(facet_spec, worker_of_subgrid, vis_count, bin_offsets, bin_fractions, observed):
    subs = lax.axis_size("sub")
    rows, cols = facet_spec.shape[2:]
    base, phases = (jnp.asarray(x) for x in phase_parts(lax.axis_size("facet")))
    routes = (along_x, along_y)
    place = places(worker_of_subgrid)
    spec = jnp.swapaxes(facet_spec, 2, 3)
    full, part, last = (RING, SUB, SUB), (RING, HALF, SUB), (FAR, SUB, SUB)
    outs = contributions(
        far_kernel, "far_parts", FAR_LIMIT, (part,) * 4 + (last,) * 2, place, spec, base, phases
    )
    arrived = [send_far(*outs[:2], along_x), send_far(*outs[2:4], along_y)]
    nears = contributions(
        near_kernel, "near_parts", NEAR_LIMIT, (full,) * 6, place, spec, base, phases, outs[4:]
    )
    arrived, nears, bin_offsets = lax.optimization_barrier((arrived, nears, bin_offsets))
    weights = kernel_weights(bin_offsets, bin_fractions)
    sums = [
        (own,) + send_near(up, down, got, route)
        for (own, up, down), got, route in zip((nears[:3], nears[3:]), arrived, routes)
    ]
    sums, weights = lax.optimization_barrier((sums, weights))
    wide = [sum(x.astype(jnp.float32) for x in parts) for parts in sums]
    sums = reduce_small([x.astype(jnp.bfloat16) for x in wide], routes[::-1])
    residual, re_part, im_part = residuals(
        vis_count, sums[0] + sums[1], *weights, observed
    )
    gathered = gather_rings((re_part, im_part), routes)
    gathered = gather_rings([in_one(parts) for parts in gathered], routes[::-1])
    kept, given = adjoint_plane(
        place, gathered[0], gathered[1], base, phases, subs, rows, cols
    )
    update = sum_rings(kept, given)
    return (residual, update[None])


def solution(mesh):
    placed = (
        P("facet", None, None, None),
        P(),
        P(("facet", "sub")),
        P(("facet", "sub"), None, None),
        P(("facet", "sub"), None, None),
        P(("facet", "sub"), None, None),
    )
    return jax.shard_map(
        on_device,
        mesh=mesh,
        in_specs=placed,
        out_specs=(P(("facet", "sub"), None, None), P("facet", None, "sub", None)),
        check_vma=False,
    )
```

```python
import math

import jax
import jax.numpy as jnp
import numpy as np
from jax import lax
from jax.experimental import pallas as pl
from jax.experimental.pallas import tpu as pltpu
from jax.sharding import PartitionSpec as P

SUB = 256
MC = 256
STEP = 64
KS = 8
BLOCK = 2048
LANES = 128
HALF = SUB // 2
RING = 4
NEAR = (0, 1, RING - 1, 2)
MIB = 1 << 20
FAR_LIMIT = 58 * MIB
NEAR_LIMIT = 36 * MIB
SMALL_LIMIT = 30 * MIB


def phase_parts(facets):
    sub_part = np.arange(SUB) - SUB // 2
    win_part = np.arange(MC) - MC // 2
    modulus = SUB * facets
    turns = 2.0 * math.pi / modulus
    residue = np.mod(win_part[:, None] * sub_part[None, :] * facets, modulus) * turns
    base = np.stack([np.cos(residue), np.sin(residue)]) * MC ** (-0.5)
    shift = np.mod(np.arange(facets)[:, None] * sub_part[None, :], modulus) * turns
    phases = np.stack([np.cos(shift), np.sin(shift)], axis=1)
    return base.astype(np.float32), phases.astype(np.float32)


def transposed_table(base, phase):
    turn_re, turn_im = phase[0, 0:1, :], phase[0, 1:2, :]
    re = base[0] * turn_re - base[1] * turn_im
    im = base[0] * turn_im + base[1] * turn_re
    return re, im


def side_by_side(*blocks):
    return jnp.concatenate(blocks, axis=1)


def stacked(*blocks):
    return jnp.concatenate(blocks, axis=0)


def f32_dot(left, right):
    return jnp.dot(left, right, preferred_element_type=jnp.float32)


def transformed(targets, place, spec, base, left, right, shifted, left_mat, right_mat):
    for part in range(2):
        shifted[part] = spec[0, part, :, STEP : STEP + shifted.shape[2]]
    a_re, a_im = (x.astype(jnp.bfloat16) for x in transposed_table(base, left))
    right_mat[...] = stacked(side_by_side(a_re, a_im), side_by_side(-a_im, a_re))
    b_re, b_im = (x.T.astype(jnp.bfloat16) for x in transposed_table(base, right))
    left_mat[...] = stacked(side_by_side(b_re, -b_im), side_by_side(b_im, b_re))
    views = []
    for across, along in targets:
        target = across * RING + along
        row_step = place[2 + 2 * target]
        first_col = pl.multiple_of(place[3 + 2 * target], STEP)
        odd = row_step % 2 == 1
        first_row = pl.multiple_of(row_step // 2 * LANES, LANES)
        parts = []
        for part in range(2):
            at_even = spec[0, part, pl.ds(first_col, MC), pl.ds(first_row, MC)]
            at_odd = shifted[part, pl.ds(first_col, MC), pl.ds(first_row, MC)]
            parts.append(jnp.where(odd, at_odd, at_even))
        views.append(side_by_side(*parts))
    halves = f32_dot(stacked(*views), right_mat[...]).astype(jnp.bfloat16)
    results = {}
    for count, target in enumerate(targets):
        half = halves[count * MC : (count + 1) * MC]
        whole = f32_dot(left_mat[...], stacked(half[:, :SUB], half[:, SUB:]))
        results[target] = whole.astype(jnp.bfloat16)
    return results


FAR = RING - 1
FAR_TARGETS = tuple((FAR, k) for k in range(RING)) + tuple((k, FAR) for k in range(FAR))
NEAR_TARGETS = tuple((i, k) for i in range(FAR) for k in range(FAR))


def far_kernel(place, spec, base, left, right, *rest):
    a_far_up, a_far_down, b_far_up, b_far_down, a_last, b_last = rest[:6]
    results = transformed(FAR_TARGETS, place, spec, base, left, right, *rest[6:])
    for k in range(RING):
        a_far_up[k] = results[FAR, k][:HALF]
        a_far_down[k] = results[FAR, k][HALF:SUB]
        b_far_up[k] = results[k, FAR][SUB : SUB + HALF]
        b_far_down[k] = results[k, FAR][SUB + HALF :]
    for k in range(FAR):
        a_last[k] = results[k, FAR][:SUB]
        b_last[k] = results[FAR, k][SUB:]


def near_kernel(place, spec, base, left, right, *rest):
    a_outs, b_outs = rest[:3], rest[3:6]
    results = transformed(NEAR_TARGETS, place, spec, base, left, right, *rest[6:])
    for i in range(FAR):
        for k in range(FAR):
            a_outs[i][k] = results[i, k][:SUB]
            b_outs[k][i] = results[i, k][SUB:]


def contributions(kernel, name, limit, shapes, place, spec, base, phases):
    cols, rows = spec.shape[2:]
    return pl.pallas_call(
        kernel,
        out_shape=tuple(jax.ShapeDtypeStruct(s, jnp.bfloat16) for s in shapes),
        grid_spec=pltpu.PrefetchScalarGridSpec(
            num_scalar_prefetch=1,
            grid=(1,),
            in_specs=[
                pl.BlockSpec((1, 2, cols, rows), lambda t, place: (0, 0, 0, 0)),
                pl.BlockSpec((2, MC, SUB), lambda t, place: (0, 0, 0)),
                pl.BlockSpec((1, 2, SUB), lambda t, place: (place[0], 0, 0)),
                pl.BlockSpec((1, 2, SUB), lambda t, place: (place[1], 0, 0)),
            ],
            out_specs=tuple(pl.BlockSpec(s, lambda t, place: (0, 0, 0)) for s in shapes),
            scratch_shapes=[
                pltpu.VMEM((2, cols, rows - STEP), jnp.bfloat16),
                pltpu.VMEM((2 * SUB, 2 * MC), jnp.bfloat16),
                pltpu.VMEM((2 * MC, 2 * SUB), jnp.bfloat16),
            ],
        ),
        compiler_params=pltpu.CompilerParams(vmem_limit_bytes=limit),
        cost_estimate=pl.CostEstimate(
            flops=8 * 2 * 2 * 512 * 512 * 256, bytes_accessed=8 * MIB, transcendentals=0
        ),
        name=name,
    )(place, spec, base, phases, phases)


def weights_kernel(offsets, fractions, u_out, v_out):
    cells = lax.broadcasted_iota(jnp.int32, (SUB, BLOCK), 0).astype(jnp.float32)
    scale = -((9.0 / KS) ** 2) / math.log(2.0)
    for axis, out in enumerate((u_out, v_out)):
        first = offsets[0, axis : axis + 1, :].astype(jnp.float32)
        inside = jnp.abs(cells - (first + 0.5 * (KS - 1))) < 0.5 * KS
        distance = cells - (first + (fractions[0, axis : axis + 1, :] + (0.5 * KS - 1.0)))
        weights = jnp.exp2(distance * distance * scale - 1.0)
        out[...] = jnp.where(inside, weights, 0.0).astype(jnp.bfloat16)


def kernel_weights(offsets, fractions):
    slots = offsets.shape[2]
    block_in = pl.BlockSpec((1, 2, BLOCK), lambda b: (0, 0, b))
    block_out = pl.BlockSpec((SUB, BLOCK), lambda b: (0, b))
    shape = jax.ShapeDtypeStruct((SUB, slots), jnp.bfloat16)
    return pl.pallas_call(
        weights_kernel,
        out_shape=(shape, shape),
        grid=(slots // BLOCK,),
        in_specs=[block_in, block_in],
        out_specs=(block_out, block_out),
        compiler_params=pltpu.CompilerParams(vmem_limit_bytes=SMALL_LIMIT),
        cost_estimate=pl.CostEstimate(
            flops=20 * SUB * slots, bytes_accessed=4 * SUB * slots, transcendentals=2 * SUB * slots
        ),
        name="kernel_weights",
    )(offsets, fractions)


def residual_kernel(count, *refs):
    grid_parts = refs[:8]
    u_in, v_in, observed, resid_out, re_out, im_out, grid, total = refs[8:]
    step = pl.program_id(0)

    @pl.when(step == 0)
    def _():
        total[...] = jnp.zeros_like(total)
        for part in range(2):
            own, *others = (ref[0].astype(jnp.float32) for ref in grid_parts[4 * part : 4 * part + 4])
            grid[part * SUB : (part + 1) * SUB] = sum(others, own).astype(jnp.bfloat16)

    u_half = u_in[...]
    v_wide = v_in[...].astype(jnp.float32)
    product = f32_dot(grid[...], u_half)
    slot = step * BLOCK + lax.broadcasted_iota(jnp.int32, (1, BLOCK), 1)
    live = slot < count[0]
    for part in range(2):
        model = jnp.sum(product[part * SUB : (part + 1) * SUB] * v_wide, axis=0, keepdims=True)
        resid = jnp.where(live, observed[0, part : part + 1, :] - model, 0.0)
        resid_out[0, part : part + 1, :] = resid
        weighted = (resid * v_wide).astype(jnp.bfloat16)
        total[part * SUB : (part + 1) * SUB] += lax.dot_general(
            u_half, weighted, (((1,), (1,)), ((), ())), preferred_element_type=jnp.float32
        )

    @pl.when(step == pl.num_programs(0) - 1)
    def _():
        re_out[0] = total[:SUB].astype(jnp.bfloat16)
        im_out[0] = total[SUB:].astype(jnp.bfloat16)


def residuals(count, grid_parts, u_weights, v_weights, observed):
    slots = observed.shape[2]
    vis_block = pl.BlockSpec((1, 2, BLOCK), lambda b, count: (0, 0, b))
    weight_block = pl.BlockSpec((SUB, BLOCK), lambda b, count: (0, b))
    whole = pl.BlockSpec((1, SUB, SUB), lambda b, count: (0, 0, 0))
    half = jax.ShapeDtypeStruct((1, SUB, SUB), jnp.bfloat16)
    return pl.pallas_call(
        residual_kernel,
        out_shape=(jax.ShapeDtypeStruct(observed.shape, jnp.float32), half, half),
        grid_spec=pltpu.PrefetchScalarGridSpec(
            num_scalar_prefetch=1,
            grid=(slots // BLOCK,),
            in_specs=[whole] * 8 + [weight_block, weight_block, vis_block],
            out_specs=(vis_block, whole, whole),
            scratch_shapes=[
                pltpu.VMEM((2 * SUB, SUB), jnp.bfloat16),
                pltpu.VMEM((2 * SUB, SUB), jnp.float32),
            ],
        ),
        compiler_params=pltpu.CompilerParams(vmem_limit_bytes=SMALL_LIMIT),
        cost_estimate=pl.CostEstimate(
            flops=4 * 512 * 256 * slots, bytes_accessed=4 * SUB * slots, transcendentals=0
        ),
        name="residuals",
    )(count, *grid_parts, u_weights, v_weights, observed)


def adjoint_kernel(place, *refs):
    re_own, re_high, re_low, re_far_low, re_far_high = refs[:5]
    im_own, im_high, im_low, im_far_low, im_far_high = refs[5:10]
    base, left, right, kept, given, plane, im_all, left_mat, right_mat = refs[10:]
    step = pl.program_id(0)
    band_rows, cols = kept.shape[2:]

    @pl.when(step == 0)
    def _():
        plane[...] = jnp.zeros_like(plane)
        im_all[0] = im_own[...]
        im_all[1] = im_high[...]
        im_all[2] = im_low[...]
        im_all[3, :, :HALF] = im_far_low[...]
        im_all[3, :, HALF:] = im_far_high[...]
        a_re, a_im = (x.astype(jnp.bfloat16) for x in transposed_table(base, left))
        left_mat[...] = stacked(side_by_side(a_re, a_im), side_by_side(-a_im, a_re))
        b_re, b_im = (x.T.astype(jnp.bfloat16) for x in transposed_table(base, right))
        right_mat[...] = stacked(side_by_side(b_re, -b_im), side_by_side(b_im, b_re))

    re_blocks = (re_own[0], re_high[0], re_low[0], stacked(re_far_low[0], re_far_high[0]))
    edge = jnp.zeros((MC, LANES), jnp.float32)
    halves = []
    for other in range(RING):
        grid = stacked(re_blocks[other], im_all[step, other])
        half = f32_dot(left_mat[...], grid).astype(jnp.bfloat16)
        halves.append(side_by_side(half[:MC], half[MC:]))
    wholes = f32_dot(stacked(*halves), right_mat[...])
    for other in range(RING):
        source = step * RING + other
        top = pl.multiple_of(place[2 + 2 * source] * STEP, STEP)
        left_col = place[3 + 2 * source]
        odd = left_col // STEP % 2
        col = pl.multiple_of(left_col // LANES * LANES, LANES)
        for part in range(2):
            whole = wholes[other * MC : (other + 1) * MC, part * MC : (part + 1) * MC]
            wide = pltpu.roll(side_by_side(whole, edge), odd * STEP, 1)
            plane[part, pl.ds(top, MC), pl.ds(col, MC + LANES)] += wide

    @pl.when(step == RING - 1)
    def _():
        for group, out in enumerate((kept, given)):
            for near in range(RING):
                band = place[2 + 2 * RING * RING + RING * group + near]
                first = pl.multiple_of(band * band_rows, 8)
                for part in range(2):
                    rows = plane[part, pl.ds(first, band_rows), :]
                    out[near, part] = rows[:, :cols].astype(jnp.bfloat16)


def adjoint_plane(place, re_parts, im_parts, base, phases, bands, rows, cols):
    facets = phases.shape[0]
    flops = facets * 2 * 2 * 512 * 512 * 256
    wide = (cols + LANES - 1) // LANES * LANES
    band_shape = (RING, 2, rows // bands, cols)
    stepped = [pl.BlockSpec((1,) + x.shape[1:], lambda t, place: (t, 0, 0)) for x in re_parts]
    whole = [pl.BlockSpec(x.shape, lambda t, place: (0, 0, 0)) for x in im_parts]
    return pl.pallas_call(
        adjoint_kernel,
        out_shape=(jax.ShapeDtypeStruct(band_shape, jnp.bfloat16),) * 2,
        grid_spec=pltpu.PrefetchScalarGridSpec(
            num_scalar_prefetch=1,
            grid=(RING,),
            in_specs=stepped
            + whole
            + [
                pl.BlockSpec((2, MC, SUB), lambda t, place: (0, 0, 0)),
                pl.BlockSpec((1, 2, SUB), lambda t, place: (place[0], 0, 0)),
                pl.BlockSpec((1, 2, SUB), lambda t, place: (place[1], 0, 0)),
            ],
            out_specs=(pl.BlockSpec(band_shape, lambda t, place: (0, 0, 0, 0)),) * 2,
            scratch_shapes=[
                pltpu.VMEM((2, rows, wide), jnp.float32),
                pltpu.VMEM((RING, RING, SUB, SUB), jnp.bfloat16),
                pltpu.VMEM((2 * MC, 2 * SUB), jnp.bfloat16),
                pltpu.VMEM((2 * SUB, 2 * MC), jnp.bfloat16),
            ],
        ),
        compiler_params=pltpu.CompilerParams(vmem_limit_bytes=SMALL_LIMIT),
        cost_estimate=pl.CostEstimate(flops=flops, bytes_accessed=8 * MIB, transcendentals=0),
        name="adjoint_plane",
    )(place, *re_parts, *im_parts, base, phases, phases)


def along_x(shift):
    return "facet", [(i, (i // RING + shift) % RING * RING + i % RING) for i in range(RING * RING)]


def along_y(shift):
    return "facet", [(i, i // RING * RING + (i % RING + shift) % RING) for i in range(RING * RING)]


def along_z(shift):
    return "sub", [(i, (i // 2 + shift) % RING * 2 + i % 2) for i in range(2 * RING)]


def move(value, route):
    return lax.ppermute(value, *route)


def near_shift(index):
    return index ^ (index >> 1)


def places(worker):
    facet = lax.axis_index("facet")
    sub = lax.axis_index("sub")
    subs = lax.axis_size("sub")
    facets = RING * RING
    entry = jnp.arange(2 + 2 * facets + 2 * RING, dtype=jnp.int32)
    target = ((entry - 2) >> 1) & (facets - 1)
    x_at = ((facet >> 2) + near_shift(target >> 2)) & (RING - 1)
    y_at = (facet + near_shift(target & (RING - 1))) & (RING - 1)
    row = (x_at * RING + y_at) * subs + sub
    ids = jnp.arange(worker.shape[0], dtype=jnp.int32)
    held = jnp.sum(jnp.where(worker[None, :] == row[:, None], ids[None, :], 0), axis=1)
    corner = jnp.where(entry & 1 == 0, held >> 3, (held & (subs - 1)) * STEP)
    table = jnp.where(entry == 0, facet, (5 * facet + 3) & (facets - 1))
    band = entry - 2 - 2 * facets
    z_at = ((sub >> 1) + near_shift(band & (RING - 1))) & (RING - 1)
    band = z_at * 2 + ((sub & 1) ^ (band >> 2 & 1))
    return jnp.where(entry < 2, table, jnp.where(entry < 2 + 2 * facets, corner, band)).astype(jnp.int32)


def with_rows(block, rows, first):
    space = [(0, 0, 0)] * block.ndim
    space[-2] = (first, block.shape[-2] - rows.shape[-2] - first, 0)
    return block + lax.pad(rows, jnp.zeros((), rows.dtype), space)


def send_far(far_up, far_down, route):
    return move(far_up, route(1)), move(far_down, route(-1))


def send_near(up, down, arrived, route):
    low, high = arrived
    return move(with_rows(up, low, 0), route(1)), move(with_rows(down, high, HALF), route(-1))


def reduce_small(blocks, routes):
    return [
        (block[:1],)
        + tuple(move(block[k : k + 1], route(NEAR[k])) for k in range(1, RING))
        for block, route in zip(blocks, routes)
    ]


def gather_rings(blocks, routes):
    parts = []
    for block, route in zip(blocks, routes):
        low, high = move(block, route(1)), move(block, route(-1))
        far = (move(low[:, :HALF], route(1)), move(high[:, HALF:], route(-1)))
        parts.append((block, high, low) + far)
    return parts


def in_one(parts):
    own, high, low, far_low, far_high = parts
    return jnp.concatenate([own, high, low, jnp.concatenate([far_low, far_high], axis=1)], axis=0)


def sum_rings(kept, given):
    swapped = lax.ppermute(given, "sub", [(i, i ^ 1) for i in range(2 * RING)])
    far = (kept[3] + swapped[3])
    low = move(far[0], along_z(1))
    high = move(far[1], along_z(-1))
    low, high = lax.optimization_barrier((low, high))
    nothing = jnp.zeros_like(low)
    up = kept[1] + swapped[1] + jnp.stack([low, nothing])
    down = kept[2] + swapped[2] + jnp.stack([nothing, high])
    low, high = move(up, along_z(1)), move(down, along_z(-1))
    wide = [x.astype(jnp.float32) for x in (kept[0], swapped[0], low, high)]
    return wide[0] + wide[1] + wide[2] + wide[3]


def on_device(facet_spec, worker_of_subgrid, vis_count, bin_offsets, bin_fractions, observed):
    subs = lax.axis_size("sub")
    rows, cols = facet_spec.shape[2:]
    base, phases = (jnp.asarray(x) for x in phase_parts(lax.axis_size("facet")))
    routes = (along_x, along_y)
    place = places(worker_of_subgrid)
    spec = jnp.swapaxes(facet_spec, 2, 3)
    part, most = (RING, HALF, SUB), (FAR, SUB, SUB)
    outs = contributions(
        far_kernel, "far_parts", FAR_LIMIT, (part,) * 4 + (most,) * 2, place, spec, base, phases
    )
    arrived = [send_far(*outs[:2], along_x), send_far(*outs[2:4], along_y)]
    nears = contributions(
        near_kernel, "near_parts", NEAR_LIMIT, (most,) * 6, place, spec, base, phases
    )
    arrived, nears, bin_offsets = lax.optimization_barrier((arrived, nears, bin_offsets))
    nears = [
        jnp.concatenate([block, outs[4 + k // 3][k % 3][None]]) for k, block in enumerate(nears)
    ]
    weights = kernel_weights(bin_offsets, bin_fractions)
    sums = [
        (own,) + send_near(up, down, got, route)
        for (own, up, down), got, route in zip((nears[:3], nears[3:]), arrived, routes)
    ]
    (own, weights) = lax.optimization_barrier((sums[0][0], weights))
    sums[0] = (own,) + sums[0][1:]
    wide = [sum(x.astype(jnp.float32) for x in parts) for parts in sums]
    sums = reduce_small([x.astype(jnp.bfloat16) for x in wide], routes[::-1])
    residual, re_part, im_part = residuals(
        vis_count, sums[0] + sums[1], *weights, observed
    )
    gathered = gather_rings((re_part, im_part), routes)
    gathered = gather_rings([in_one(parts) for parts in gathered], routes[::-1])
    kept, given = adjoint_plane(
        place, gathered[0], gathered[1], base, phases, subs, rows, cols
    )
    update = sum_rings(kept, given)
    return (residual, update[None])


def solution(mesh):
    placed = (
        P("facet", None, None, None),
        P(),
        P(("facet", "sub")),
        P(("facet", "sub"), None, None),
        P(("facet", "sub"), None, None),
        P(("facet", "sub"), None, None),
    )
    return jax.shard_map(
        on_device,
        mesh=mesh,
        in_specs=placed,
        out_specs=(P(("facet", "sub"), None, None), P("facet", None, "sub", None)),
        check_vma=False,
    )
```

```python
import math

import jax
import jax.numpy as jnp
import numpy as np
from jax import lax
from jax.experimental import pallas as pl
from jax.experimental.pallas import tpu as pltpu
from jax.sharding import PartitionSpec as P

SUB = 256
MC = 256
STEP = 64
KS = 8
BLOCK = 2048
LANES = 128
HALF = SUB // 2
RING = 4
NEAR = (0, 1, RING - 1, 2)
MIB = 1 << 20
FAR_LIMIT = 58 * MIB
NEAR_LIMIT = 36 * MIB
SMALL_LIMIT = 30 * MIB


def phase_parts(facets):
    sub_part = np.arange(SUB) - SUB // 2
    win_part = np.arange(MC) - MC // 2
    modulus = SUB * facets
    turns = 2.0 * math.pi / modulus
    residue = np.mod(win_part[:, None] * sub_part[None, :] * facets, modulus) * turns
    base = np.stack([np.cos(residue), np.sin(residue)]) * MC ** (-0.5)
    shift = np.mod(np.arange(facets)[:, None] * sub_part[None, :], modulus) * turns
    phases = np.stack([np.cos(shift), np.sin(shift)], axis=1)
    return base.astype(np.float32), phases.astype(np.float32)


def transposed_table(base, phase):
    turn_re, turn_im = phase[0, 0:1, :], phase[0, 1:2, :]
    re = base[0] * turn_re - base[1] * turn_im
    im = base[0] * turn_im + base[1] * turn_re
    return re, im


def side_by_side(*blocks):
    return jnp.concatenate(blocks, axis=1)


def stacked(*blocks):
    return jnp.concatenate(blocks, axis=0)


def f32_dot(left, right):
    return jnp.dot(left, right, preferred_element_type=jnp.float32)


def set_tables(base, left, right, left_mat, right_mat):
    a_re, a_im = (x.astype(jnp.bfloat16) for x in transposed_table(base, left))
    right_mat[...] = stacked(side_by_side(a_re, a_im), side_by_side(-a_im, a_re))
    b_re, b_im = (x.T.astype(jnp.bfloat16) for x in transposed_table(base, right))
    left_mat[...] = stacked(side_by_side(b_re, -b_im), side_by_side(b_im, b_re))


def transformed(targets, place, spec, shifted, left_mat, right_mat):
    for part in range(2):
        shifted[part] = spec[0, part, :, STEP : STEP + shifted.shape[2]]
    views = []
    for across, along in targets:
        target = across * RING + along
        row_step = place[2 + 2 * target]
        first_col = pl.multiple_of(place[3 + 2 * target], STEP)
        odd = row_step % 2 == 1
        first_row = pl.multiple_of(row_step // 2 * LANES, LANES)
        parts = []
        for part in range(2):
            at_even = spec[0, part, pl.ds(first_col, MC), pl.ds(first_row, MC)]
            at_odd = shifted[part, pl.ds(first_col, MC), pl.ds(first_row, MC)]
            parts.append(jnp.where(odd, at_odd, at_even))
        views.append(side_by_side(*parts))
    halves = f32_dot(stacked(*views), right_mat[...]).astype(jnp.bfloat16)
    results = {}
    for count, target in enumerate(targets):
        half = halves[count * MC : (count + 1) * MC]
        whole = f32_dot(left_mat[...], stacked(half[:, :SUB], half[:, SUB:]))
        results[target] = whole.astype(jnp.bfloat16)
    return results


FAR = RING - 1
FAR_TARGETS = tuple((FAR, k) for k in range(RING)) + tuple((k, FAR) for k in range(FAR))
NEAR_TARGETS = tuple((i, k) for i in range(FAR) for k in range(FAR))


def set_places(worker, place, held):
    facet = lax.axis_index("facet")
    sub = lax.axis_index("sub")
    facets, subs = RING * RING, 2 * RING

    def look(subgrid, carry):
        row = worker[subgrid]
        held[jnp.where(row & (subs - 1) == sub, row >> 3, facets)] = subgrid
        return carry

    lax.fori_loop(0, facets * subs, look, 0, unroll=8)
    place[0] = facet
    place[1] = (5 * facet + 3) & (facets - 1)
    for across in range(RING):
        for along in range(RING):
            x_at = ((facet >> 2) + NEAR[across]) & (RING - 1)
            y_at = (facet + NEAR[along]) & (RING - 1)
            subgrid = held[x_at * RING + y_at]
            entry = 2 + 2 * (across * RING + along)
            place[entry] = subgrid >> 3
            place[entry + 1] = (subgrid & (subs - 1)) * STEP
    for group in range(2):
        for near in range(RING):
            z_at = ((sub >> 1) + NEAR[near]) & (RING - 1)
            place[2 + 2 * facets + RING * group + near] = z_at * 2 + ((sub & 1) ^ group)


def far_kernel(worker, spec, base, phases, *rest):
    a_far_up, a_far_down, b_far_up, b_far_down, a_last, b_last, place = rest[:7]
    held, spec_copy, arrival, shifted, left_mat, right_mat = rest[7:]
    load = pltpu.make_async_copy(spec, spec_copy, arrival)
    load.start()
    set_places(worker, place, held)
    left, right = phases[pl.ds(place[0], 1)], phases[pl.ds(place[1], 1)]
    set_tables(base, left, right, left_mat, right_mat)
    load.wait()
    results = transformed(FAR_TARGETS, place, spec_copy, shifted, left_mat, right_mat)
    for k in range(RING):
        a_far_up[k] = results[FAR, k][:HALF]
        a_far_down[k] = results[FAR, k][HALF:SUB]
        b_far_up[k] = results[k, FAR][SUB : SUB + HALF]
        b_far_down[k] = results[k, FAR][SUB + HALF :]
    for k in range(FAR):
        a_last[k] = results[k, FAR][:SUB]
        b_last[k] = results[FAR, k][SUB:]


def near_kernel(place, spec, base, left, right, *rest):
    a_outs, b_outs = rest[:3], rest[3:6]
    shifted, left_mat, right_mat = rest[6:]
    set_tables(base, left, right, left_mat, right_mat)
    results = transformed(NEAR_TARGETS, place, spec, shifted, left_mat, right_mat)
    for i in range(FAR):
        for k in range(FAR):
            a_outs[i][k] = results[i, k][:SUB]
            b_outs[k][i] = results[i, k][SUB:]


def cut_scratch(cols, rows):
    return [
        pltpu.VMEM((2, cols, rows - STEP), jnp.bfloat16),
        pltpu.VMEM((2 * SUB, 2 * MC), jnp.bfloat16),
        pltpu.VMEM((2 * MC, 2 * SUB), jnp.bfloat16),
    ]


CUT_COST = pl.CostEstimate(
    flops=8 * 2 * 2 * 512 * 512 * 256, bytes_accessed=8 * MIB, transcendentals=0
)


def whole_block(shape):
    return pl.BlockSpec(shape, lambda t, scalars: (0,) * len(shape))


def far_parts(worker, spec, base, phases, shapes):
    cols, rows = spec.shape[2:]
    entries = 2 + 2 * RING * RING + 2 * RING
    return pl.pallas_call(
        far_kernel,
        out_shape=tuple(jax.ShapeDtypeStruct(s, jnp.bfloat16) for s in shapes)
        + (jax.ShapeDtypeStruct((entries,), jnp.int32),),
        grid_spec=pltpu.PrefetchScalarGridSpec(
            num_scalar_prefetch=1,
            grid=(1,),
            in_specs=[
                pl.BlockSpec(memory_space=pl.ANY),
                whole_block(base.shape),
                whole_block(phases.shape),
            ],
            out_specs=tuple(whole_block(s) for s in shapes)
            + (pl.BlockSpec(memory_space=pltpu.SMEM),),
            scratch_shapes=[
                pltpu.SMEM((2 * RING * RING,), jnp.int32),
                pltpu.VMEM((1, 2, cols, rows), jnp.bfloat16),
                pltpu.SemaphoreType.DMA,
            ]
            + cut_scratch(cols, rows),
        ),
        compiler_params=pltpu.CompilerParams(vmem_limit_bytes=FAR_LIMIT),
        cost_estimate=CUT_COST,
        name="far_parts",
    )(worker, spec, base, phases)


def near_parts(place, spec, base, phases, shapes):
    cols, rows = spec.shape[2:]
    return pl.pallas_call(
        near_kernel,
        out_shape=tuple(jax.ShapeDtypeStruct(s, jnp.bfloat16) for s in shapes),
        grid_spec=pltpu.PrefetchScalarGridSpec(
            num_scalar_prefetch=1,
            grid=(1,),
            in_specs=[
                whole_block(spec.shape),
                whole_block(base.shape),
                pl.BlockSpec((1, 2, SUB), lambda t, place: (place[0], 0, 0)),
                pl.BlockSpec((1, 2, SUB), lambda t, place: (place[1], 0, 0)),
            ],
            out_specs=tuple(whole_block(s) for s in shapes),
            scratch_shapes=cut_scratch(cols, rows),
        ),
        compiler_params=pltpu.CompilerParams(vmem_limit_bytes=NEAR_LIMIT),
        cost_estimate=CUT_COST,
        name="near_parts",
    )(place, spec, base, phases, phases)


def weights_kernel(offsets, fractions, u_out, v_out):
    cells = lax.broadcasted_iota(jnp.int32, (SUB, BLOCK), 0).astype(jnp.float32)
    scale = -((9.0 / KS) ** 2) / math.log(2.0)
    for axis, out in enumerate((u_out, v_out)):
        first = offsets[0, axis : axis + 1, :].astype(jnp.float32)
        inside = jnp.abs(cells - (first + 0.5 * (KS - 1))) < 0.5 * KS
        distance = cells - (first + (fractions[0, axis : axis + 1, :] + (0.5 * KS - 1.0)))
        weights = jnp.exp2(distance * distance * scale - 1.0)
        out[...] = jnp.where(inside, weights, 0.0).astype(jnp.bfloat16)


def kernel_weights(offsets, fractions):
    slots = offsets.shape[2]
    block_in = pl.BlockSpec((1, 2, BLOCK), lambda b: (0, 0, b))
    block_out = pl.BlockSpec((SUB, BLOCK), lambda b: (0, b))
    shape = jax.ShapeDtypeStruct((SUB, slots), jnp.bfloat16)
    return pl.pallas_call(
        weights_kernel,
        out_shape=(shape, shape),
        grid=(slots // BLOCK,),
        in_specs=[block_in, block_in],
        out_specs=(block_out, block_out),
        compiler_params=pltpu.CompilerParams(vmem_limit_bytes=SMALL_LIMIT),
        cost_estimate=pl.CostEstimate(
            flops=20 * SUB * slots, bytes_accessed=4 * SUB * slots, transcendentals=2 * SUB * slots
        ),
        name="kernel_weights",
    )(offsets, fractions)


def residual_kernel(count, *refs):
    grid_parts = refs[:8]
    u_in, v_in, observed, resid_out, re_out, im_out, grid, total = refs[8:]
    step = pl.program_id(0)

    @pl.when(step == 0)
    def _():
        total[...] = jnp.zeros_like(total)
        for part in range(2):
            own, *others = (ref[0].astype(jnp.float32) for ref in grid_parts[4 * part : 4 * part + 4])
            grid[part * SUB : (part + 1) * SUB] = sum(others, own).astype(jnp.bfloat16)

    u_half = u_in[...]
    v_wide = v_in[...].astype(jnp.float32)
    product = f32_dot(grid[...], u_half)
    slot = step * BLOCK + lax.broadcasted_iota(jnp.int32, (1, BLOCK), 1)
    live = slot < count[0]
    for part in range(2):
        model = jnp.sum(product[part * SUB : (part + 1) * SUB] * v_wide, axis=0, keepdims=True)
        resid = jnp.where(live, observed[0, part : part + 1, :] - model, 0.0)
        resid_out[0, part : part + 1, :] = resid
        weighted = (resid * v_wide).astype(jnp.bfloat16)
        total[part * SUB : (part + 1) * SUB] += lax.dot_general(
            u_half, weighted, (((1,), (1,)), ((), ())), preferred_element_type=jnp.float32
        )

    @pl.when(step == pl.num_programs(0) - 1)
    def _():
        re_out[0] = total[:SUB].astype(jnp.bfloat16)
        im_out[0] = total[SUB:].astype(jnp.bfloat16)


def residuals(count, grid_parts, u_weights, v_weights, observed):
    slots = observed.shape[2]
    vis_block = pl.BlockSpec((1, 2, BLOCK), lambda b, count: (0, 0, b))
    weight_block = pl.BlockSpec((SUB, BLOCK), lambda b, count: (0, b))
    whole = pl.BlockSpec((1, SUB, SUB), lambda b, count: (0, 0, 0))
    half = jax.ShapeDtypeStruct((1, SUB, SUB), jnp.bfloat16)
    return pl.pallas_call(
        residual_kernel,
        out_shape=(jax.ShapeDtypeStruct(observed.shape, jnp.float32), half, half),
        grid_spec=pltpu.PrefetchScalarGridSpec(
            num_scalar_prefetch=1,
            grid=(slots // BLOCK,),
            in_specs=[whole] * 8 + [weight_block, weight_block, vis_block],
            out_specs=(vis_block, whole, whole),
            scratch_shapes=[
                pltpu.VMEM((2 * SUB, SUB), jnp.bfloat16),
                pltpu.VMEM((2 * SUB, SUB), jnp.float32),
            ],
        ),
        compiler_params=pltpu.CompilerParams(vmem_limit_bytes=SMALL_LIMIT),
        cost_estimate=pl.CostEstimate(
            flops=4 * 512 * 256 * slots, bytes_accessed=4 * SUB * slots, transcendentals=0
        ),
        name="residuals",
    )(count, *grid_parts, u_weights, v_weights, observed)


def adjoint_kernel(place, *refs):
    re_own, re_high, re_low, re_far_low, re_far_high = refs[:5]
    im_own, im_high, im_low, im_far_low, im_far_high = refs[5:10]
    base, left, right, kept, given, plane, im_all, left_mat, right_mat = refs[10:]
    step = pl.program_id(0)
    band_rows, cols = kept.shape[2:]

    @pl.when(step == 0)
    def _():
        plane[...] = jnp.zeros_like(plane)
        im_all[0] = im_own[...]
        im_all[1] = im_high[...]
        im_all[2] = im_low[...]
        im_all[3, :, :HALF] = im_far_low[...]
        im_all[3, :, HALF:] = im_far_high[...]
        a_re, a_im = (x.astype(jnp.bfloat16) for x in transposed_table(base, left))
        left_mat[...] = stacked(side_by_side(a_re, a_im), side_by_side(-a_im, a_re))
        b_re, b_im = (x.T.astype(jnp.bfloat16) for x in transposed_table(base, right))
        right_mat[...] = stacked(side_by_side(b_re, -b_im), side_by_side(b_im, b_re))

    re_blocks = (re_own[0], re_high[0], re_low[0], stacked(re_far_low[0], re_far_high[0]))
    edge = jnp.zeros((MC, LANES), jnp.float32)
    halves = []
    for other in range(RING):
        grid = stacked(re_blocks[other], im_all[step, other])
        half = f32_dot(left_mat[...], grid).astype(jnp.bfloat16)
        halves.append(side_by_side(half[:MC], half[MC:]))
    wholes = f32_dot(stacked(*halves), right_mat[...])
    for other in range(RING):
        source = step * RING + other
        top = pl.multiple_of(place[2 + 2 * source] * STEP, STEP)
        left_col = place[3 + 2 * source]
        odd = left_col // STEP % 2
        col = pl.multiple_of(left_col // LANES * LANES, LANES)
        for part in range(2):
            whole = wholes[other * MC : (other + 1) * MC, part * MC : (part + 1) * MC]
            wide = pltpu.roll(side_by_side(whole, edge), odd * STEP, 1)
            plane[part, pl.ds(top, MC), pl.ds(col, MC + LANES)] += wide

    @pl.when(step == RING - 1)
    def _():
        for group, out in enumerate((kept, given)):
            for near in range(RING):
                band = place[2 + 2 * RING * RING + RING * group + near]
                first = pl.multiple_of(band * band_rows, 8)
                for part in range(2):
                    rows = plane[part, pl.ds(first, band_rows), :]
                    out[near, part] = rows[:, :cols].astype(jnp.bfloat16)


def adjoint_plane(place, re_parts, im_parts, base, phases, bands, rows, cols):
    facets = phases.shape[0]
    flops = facets * 2 * 2 * 512 * 512 * 256
    wide = (cols + LANES - 1) // LANES * LANES
    band_shape = (RING, 2, rows // bands, cols)
    stepped = [pl.BlockSpec((1,) + x.shape[1:], lambda t, place: (t, 0, 0)) for x in re_parts]
    whole = [pl.BlockSpec(x.shape, lambda t, place: (0, 0, 0)) for x in im_parts]
    return pl.pallas_call(
        adjoint_kernel,
        out_shape=(jax.ShapeDtypeStruct(band_shape, jnp.bfloat16),) * 2,
        grid_spec=pltpu.PrefetchScalarGridSpec(
            num_scalar_prefetch=1,
            grid=(RING,),
            in_specs=stepped
            + whole
            + [
                pl.BlockSpec((2, MC, SUB), lambda t, place: (0, 0, 0)),
                pl.BlockSpec((1, 2, SUB), lambda t, place: (place[0], 0, 0)),
                pl.BlockSpec((1, 2, SUB), lambda t, place: (place[1], 0, 0)),
            ],
            out_specs=(pl.BlockSpec(band_shape, lambda t, place: (0, 0, 0, 0)),) * 2,
            scratch_shapes=[
                pltpu.VMEM((2, rows, wide), jnp.float32),
                pltpu.VMEM((RING, RING, SUB, SUB), jnp.bfloat16),
                pltpu.VMEM((2 * MC, 2 * SUB), jnp.bfloat16),
                pltpu.VMEM((2 * SUB, 2 * MC), jnp.bfloat16),
            ],
        ),
        compiler_params=pltpu.CompilerParams(vmem_limit_bytes=SMALL_LIMIT),
        cost_estimate=pl.CostEstimate(flops=flops, bytes_accessed=8 * MIB, transcendentals=0),
        name="adjoint_plane",
    )(place, *re_parts, *im_parts, base, phases, phases)


def along_x(shift):
    return "facet", [(i, (i // RING + shift) % RING * RING + i % RING) for i in range(RING * RING)]


def along_y(shift):
    return "facet", [(i, i // RING * RING + (i % RING + shift) % RING) for i in range(RING * RING)]


def along_z(shift):
    return "sub", [(i, (i // 2 + shift) % RING * 2 + i % 2) for i in range(2 * RING)]


def move(value, route):
    return lax.ppermute(value, *route)


def with_rows(block, rows, first):
    space = [(0, 0, 0)] * block.ndim
    space[-2] = (first, block.shape[-2] - rows.shape[-2] - first, 0)
    return block + lax.pad(rows, jnp.zeros((), rows.dtype), space)


def send_far(far_up, far_down, route):
    return move(far_up, route(1)), move(far_down, route(-1))


def send_near(up, down, arrived, route):
    low, high = arrived
    return move(with_rows(up, low, 0), route(1)), move(with_rows(down, high, HALF), route(-1))


def reduce_small(blocks, routes):
    return [
        (block[:1],)
        + tuple(move(block[k : k + 1], route(NEAR[k])) for k in range(1, RING))
        for block, route in zip(blocks, routes)
    ]


def gather_rings(blocks, routes):
    parts = []
    for block, route in zip(blocks, routes):
        low, high = move(block, route(1)), move(block, route(-1))
        far = (move(low[:, :HALF], route(1)), move(high[:, HALF:], route(-1)))
        parts.append((block, high, low) + far)
    return parts


def in_one(parts):
    own, high, low, far_low, far_high = parts
    return jnp.concatenate([own, high, low, jnp.concatenate([far_low, far_high], axis=1)], axis=0)


def sum_rings(kept, given):
    swapped = lax.ppermute(given, "sub", [(i, i ^ 1) for i in range(2 * RING)])
    chip = kept + swapped
    low = move(chip[3, 0], along_z(1))
    high = move(chip[3, 1], along_z(-1))
    up_im = move(chip[1, 1], along_z(1))
    down_re = move(chip[2, 0], along_z(-1))
    up_re = move(chip[1, 0] + low, along_z(1))
    down_im = move(chip[2, 1] + high, along_z(-1))
    own = kept[0].astype(jnp.float32) + swapped[0].astype(jnp.float32)
    re = own[0] + up_re.astype(jnp.float32) + down_re.astype(jnp.float32)
    im = own[1] + up_im.astype(jnp.float32) + down_im.astype(jnp.float32)
    return jnp.stack([re, im])


def on_device(facet_spec, worker_of_subgrid, vis_count, bin_offsets, bin_fractions, observed):
    subs = lax.axis_size("sub")
    rows, cols = facet_spec.shape[2:]
    base, phases = (jnp.asarray(x) for x in phase_parts(lax.axis_size("facet")))
    routes = (along_x, along_y)
    spec = jnp.swapaxes(facet_spec, 2, 3)
    part, most = (RING, HALF, SUB), (FAR, SUB, SUB)
    *outs, place = far_parts(worker_of_subgrid, spec, base, phases, (part,) * 4 + (most,) * 2)
    arrived = [send_far(*outs[:2], along_x), send_far(*outs[2:4], along_y)]
    nears = near_parts(place, spec, base, phases, (most,) * 6)
    arrived, nears, bin_offsets = lax.optimization_barrier((arrived, nears, bin_offsets))
    nears = [
        jnp.concatenate([block, outs[4 + k // 3][k % 3][None]]) for k, block in enumerate(nears)
    ]
    weights = kernel_weights(bin_offsets, bin_fractions)
    sums = [
        (own,) + send_near(up, down, got, route)
        for (own, up, down), got, route in zip((nears[:3], nears[3:]), arrived, routes)
    ]
    (own, weights) = lax.optimization_barrier((sums[0][0], weights))
    sums[0] = (own,) + sums[0][1:]
    wide = [sum(x.astype(jnp.float32) for x in parts) for parts in sums]
    sums = reduce_small([x.astype(jnp.bfloat16) for x in wide], routes[::-1])
    residual, re_part, im_part = residuals(
        vis_count, sums[0] + sums[1], *weights, observed
    )
    gathered = gather_rings((re_part, im_part), routes)
    gathered = gather_rings([in_one(parts) for parts in gathered], routes[::-1])
    kept, given = adjoint_plane(
        place, gathered[0], gathered[1], base, phases, subs, rows, cols
    )
    update = sum_rings(kept, given)
    return (residual, update[None])


def solution(mesh):
    placed = (
        P("facet", None, None, None),
        P(),
        P(("facet", "sub")),
        P(("facet", "sub"), None, None),
        P(("facet", "sub"), None, None),
        P(("facet", "sub"), None, None),
    )
    return jax.shard_map(
        on_device,
        mesh=mesh,
        in_specs=placed,
        out_specs=(P(("facet", "sub"), None, None), P("facet", None, "sub", None)),
        check_vma=False,
    )
```

```python
import math

import jax
import jax.numpy as jnp
import numpy as np
from jax import lax
from jax.experimental import pallas as pl
from jax.experimental.pallas import tpu as pltpu
from jax.sharding import PartitionSpec as P

SUB = 256
MC = 256
STEP = 64
KS = 8
BLOCK = 4096
LANES = 128
HALF = SUB // 2
RING = 4
NEAR = (0, 1, RING - 1, 2)
MIB = 1 << 20
FAR_LIMIT = 58 * MIB
NEAR_LIMIT = 36 * MIB
SMALL_LIMIT = 30 * MIB


def phase_parts(facets):
    sub_part = np.arange(SUB) - SUB // 2
    win_part = np.arange(MC) - MC // 2
    modulus = SUB * facets
    turns = 2.0 * math.pi / modulus
    residue = np.mod(win_part[:, None] * sub_part[None, :] * facets, modulus) * turns
    base = np.stack([np.cos(residue), np.sin(residue)]) * MC ** (-0.5)
    shift = np.mod(np.arange(facets)[:, None] * sub_part[None, :], modulus) * turns
    phases = np.stack([np.cos(shift), np.sin(shift)], axis=1)
    return base.astype(np.float32), phases.astype(np.float32)


def transposed_table(base, phase):
    turn_re, turn_im = phase[0, 0:1, :], phase[0, 1:2, :]
    re = base[0] * turn_re - base[1] * turn_im
    im = base[0] * turn_im + base[1] * turn_re
    return re, im


def side_by_side(*blocks):
    return jnp.concatenate(blocks, axis=1)


def stacked(*blocks):
    return jnp.concatenate(blocks, axis=0)


def f32_dot(left, right):
    return jnp.dot(left, right, preferred_element_type=jnp.float32)


def set_tables(base, left, right, left_mat, right_mat):
    a_re, a_im = (x.astype(jnp.bfloat16) for x in transposed_table(base, left))
    right_mat[...] = stacked(side_by_side(a_re, a_im), side_by_side(-a_im, a_re))
    b_re, b_im = (x.T.astype(jnp.bfloat16) for x in transposed_table(base, right))
    left_mat[...] = stacked(side_by_side(b_re, -b_im), side_by_side(b_im, b_re))


def transformed(targets, place, spec, shifted, left_mat, right_mat):
    for part in range(2):
        shifted[part] = spec[0, part, :, STEP : STEP + shifted.shape[2]]
    views = []
    for across, along in targets:
        target = across * RING + along
        row_step = place[2 + 2 * target]
        first_col = pl.multiple_of(place[3 + 2 * target], STEP)
        odd = row_step % 2 == 1
        first_row = pl.multiple_of(row_step // 2 * LANES, LANES)
        parts = []
        for part in range(2):
            at_even = spec[0, part, pl.ds(first_col, MC), pl.ds(first_row, MC)]
            at_odd = shifted[part, pl.ds(first_col, MC), pl.ds(first_row, MC)]
            parts.append(jnp.where(odd, at_odd, at_even))
        views.append(side_by_side(*parts))
    halves = f32_dot(stacked(*views), right_mat[...]).astype(jnp.bfloat16)
    results = {}
    for count, target in enumerate(targets):
        half = halves[count * MC : (count + 1) * MC]
        whole = f32_dot(left_mat[...], stacked(half[:, :SUB], half[:, SUB:]))
        results[target] = whole.astype(jnp.bfloat16)
    return results


FAR = RING - 1
FAR_TARGETS = tuple((FAR, k) for k in range(RING)) + tuple((k, FAR) for k in range(FAR))
NEAR_TARGETS = tuple((i, k) for i in range(FAR) for k in range(FAR))


def set_places(worker, place, held):
    facet = lax.axis_index("facet")
    sub = lax.axis_index("sub")
    facets, subs = RING * RING, 2 * RING

    def look(subgrid, carry):
        row = worker[subgrid]
        held[jnp.where(row & (subs - 1) == sub, row >> 3, facets)] = subgrid
        return carry

    lax.fori_loop(0, facets * subs, look, 0, unroll=8)
    place[0] = facet
    place[1] = (5 * facet + 3) & (facets - 1)
    for across in range(RING):
        for along in range(RING):
            x_at = ((facet >> 2) + NEAR[across]) & (RING - 1)
            y_at = (facet + NEAR[along]) & (RING - 1)
            subgrid = held[x_at * RING + y_at]
            entry = 2 + 2 * (across * RING + along)
            place[entry] = subgrid >> 3
            place[entry + 1] = (subgrid & (subs - 1)) * STEP
    for group in range(2):
        for near in range(RING):
            z_at = ((sub >> 1) + NEAR[near]) & (RING - 1)
            place[2 + 2 * facets + RING * group + near] = z_at * 2 + ((sub & 1) ^ group)


def far_kernel(worker, spec, base, phases, *rest):
    a_far_up, a_far_down, b_far_up, b_far_down, a_last, b_last, place = rest[:7]
    held, spec_copy, arrival, shifted, left_mat, right_mat = rest[7:]
    load = pltpu.make_async_copy(spec, spec_copy, arrival)
    load.start()
    set_places(worker, place, held)
    left, right = phases[pl.ds(place[0], 1)], phases[pl.ds(place[1], 1)]
    set_tables(base, left, right, left_mat, right_mat)
    load.wait()
    results = transformed(FAR_TARGETS, place, spec_copy, shifted, left_mat, right_mat)
    for k in range(RING):
        a_far_up[k] = results[FAR, k][:HALF]
        a_far_down[k] = results[FAR, k][HALF:SUB]
        b_far_up[k] = results[k, FAR][SUB : SUB + HALF]
        b_far_down[k] = results[k, FAR][SUB + HALF :]
    for k in range(FAR):
        a_last[k] = results[k, FAR][:SUB]
        b_last[k] = results[FAR, k][SUB:]


def near_kernel(place, spec, base, left, right, *rest):
    a_outs, b_outs = rest[:3], rest[3:6]
    shifted, left_mat, right_mat = rest[6:]
    set_tables(base, left, right, left_mat, right_mat)
    results = transformed(NEAR_TARGETS, place, spec, shifted, left_mat, right_mat)
    for i in range(FAR):
        for k in range(FAR):
            a_outs[i][k] = results[i, k][:SUB]
            b_outs[k][i] = results[i, k][SUB:]


def cut_scratch(cols, rows):
    return [
        pltpu.VMEM((2, cols, rows - STEP), jnp.bfloat16),
        pltpu.VMEM((2 * SUB, 2 * MC), jnp.bfloat16),
        pltpu.VMEM((2 * MC, 2 * SUB), jnp.bfloat16),
    ]


CUT_COST = pl.CostEstimate(
    flops=8 * 2 * 2 * 512 * 512 * 256, bytes_accessed=8 * MIB, transcendentals=0
)


def whole_block(shape):
    return pl.BlockSpec(shape, lambda t, scalars: (0,) * len(shape))


def far_parts(worker, spec, base, phases, shapes):
    cols, rows = spec.shape[2:]
    entries = 2 + 2 * RING * RING + 2 * RING
    return pl.pallas_call(
        far_kernel,
        out_shape=tuple(jax.ShapeDtypeStruct(s, jnp.bfloat16) for s in shapes)
        + (jax.ShapeDtypeStruct((entries,), jnp.int32),),
        grid_spec=pltpu.PrefetchScalarGridSpec(
            num_scalar_prefetch=1,
            grid=(1,),
            in_specs=[
                pl.BlockSpec(memory_space=pl.ANY),
                whole_block(base.shape),
                whole_block(phases.shape),
            ],
            out_specs=tuple(whole_block(s) for s in shapes)
            + (pl.BlockSpec(memory_space=pltpu.SMEM),),
            scratch_shapes=[
                pltpu.SMEM((2 * RING * RING,), jnp.int32),
                pltpu.VMEM((1, 2, cols, rows), jnp.bfloat16),
                pltpu.SemaphoreType.DMA,
            ]
            + cut_scratch(cols, rows),
        ),
        compiler_params=pltpu.CompilerParams(vmem_limit_bytes=FAR_LIMIT),
        cost_estimate=CUT_COST,
        name="far_parts",
    )(worker, spec, base, phases)


def near_parts(place, spec, base, phases, shapes):
    cols, rows = spec.shape[2:]
    return pl.pallas_call(
        near_kernel,
        out_shape=tuple(jax.ShapeDtypeStruct(s, jnp.bfloat16) for s in shapes),
        grid_spec=pltpu.PrefetchScalarGridSpec(
            num_scalar_prefetch=1,
            grid=(1,),
            in_specs=[
                whole_block(spec.shape),
                whole_block(base.shape),
                pl.BlockSpec((1, 2, SUB), lambda t, place: (place[0], 0, 0)),
                pl.BlockSpec((1, 2, SUB), lambda t, place: (place[1], 0, 0)),
            ],
            out_specs=tuple(whole_block(s) for s in shapes),
            scratch_shapes=cut_scratch(cols, rows),
        ),
        compiler_params=pltpu.CompilerParams(vmem_limit_bytes=NEAR_LIMIT),
        cost_estimate=CUT_COST,
        name="near_parts",
    )(place, spec, base, phases, phases)


def weights_kernel(offsets, fractions, u_out, v_out):
    cells = lax.broadcasted_iota(jnp.int32, (SUB, BLOCK), 0).astype(jnp.float32)
    scale = -((9.0 / KS) ** 2) / math.log(2.0)
    for axis, out in enumerate((u_out, v_out)):
        first = offsets[0, axis : axis + 1, :].astype(jnp.float32)
        inside = jnp.abs(cells - (first + 0.5 * (KS - 1))) < 0.5 * KS
        distance = cells - (first + (fractions[0, axis : axis + 1, :] + (0.5 * KS - 1.0)))
        weights = jnp.exp2(distance * distance * scale - 1.0)
        out[...] = jnp.where(inside, weights, 0.0).astype(jnp.bfloat16)


def kernel_weights(offsets, fractions):
    slots = offsets.shape[2]
    block_in = pl.BlockSpec((1, 2, BLOCK), lambda b: (0, 0, b))
    block_out = pl.BlockSpec((SUB, BLOCK), lambda b: (0, b))
    shape = jax.ShapeDtypeStruct((SUB, slots), jnp.bfloat16)
    return pl.pallas_call(
        weights_kernel,
        out_shape=(shape, shape),
        grid=(slots // BLOCK,),
        in_specs=[block_in, block_in],
        out_specs=(block_out, block_out),
        compiler_params=pltpu.CompilerParams(vmem_limit_bytes=SMALL_LIMIT),
        cost_estimate=pl.CostEstimate(
            flops=20 * SUB * slots, bytes_accessed=4 * SUB * slots, transcendentals=2 * SUB * slots
        ),
        name="kernel_weights",
    )(offsets, fractions)


def residual_kernel(count, *refs):
    grid_parts = refs[:8]
    u_in, v_in, observed, resid_out, re_out, im_out, grid, total = refs[8:]
    step = pl.program_id(0)

    @pl.when(step == 0)
    def _():
        total[...] = jnp.zeros_like(total)
        for part in range(2):
            own, *others = (ref[0].astype(jnp.float32) for ref in grid_parts[4 * part : 4 * part + 4])
            grid[part * SUB : (part + 1) * SUB] = sum(others, own).astype(jnp.bfloat16)

    u_half = u_in[...]
    v_wide = v_in[...].astype(jnp.float32)
    product = f32_dot(grid[...], u_half)
    slot = step * BLOCK + lax.broadcasted_iota(jnp.int32, (1, BLOCK), 1)
    live = slot < count[0]
    for part in range(2):
        model = jnp.sum(product[part * SUB : (part + 1) * SUB] * v_wide, axis=0, keepdims=True)
        resid = jnp.where(live, observed[0, part : part + 1, :] - model, 0.0)
        resid_out[0, part : part + 1, :] = resid
        weighted = (resid * v_wide).astype(jnp.bfloat16)
        total[part * SUB : (part + 1) * SUB] += lax.dot_general(
            u_half, weighted, (((1,), (1,)), ((), ())), preferred_element_type=jnp.float32
        )

    @pl.when(step == pl.num_programs(0) - 1)
    def _():
        re_out[0] = total[:SUB].astype(jnp.bfloat16)
        im_out[0] = total[SUB:].astype(jnp.bfloat16)


def residuals(count, grid_parts, u_weights, v_weights, observed):
    slots = observed.shape[2]
    vis_block = pl.BlockSpec((1, 2, BLOCK), lambda b, count: (0, 0, b))
    weight_block = pl.BlockSpec((SUB, BLOCK), lambda b, count: (0, b))
    whole = pl.BlockSpec((1, SUB, SUB), lambda b, count: (0, 0, 0))
    half = jax.ShapeDtypeStruct((1, SUB, SUB), jnp.bfloat16)
    return pl.pallas_call(
        residual_kernel,
        out_shape=(jax.ShapeDtypeStruct(observed.shape, jnp.float32), half, half),
        grid_spec=pltpu.PrefetchScalarGridSpec(
            num_scalar_prefetch=1,
            grid=(slots // BLOCK,),
            in_specs=[whole] * 8 + [weight_block, weight_block, vis_block],
            out_specs=(vis_block, whole, whole),
            scratch_shapes=[
                pltpu.VMEM((2 * SUB, SUB), jnp.bfloat16),
                pltpu.VMEM((2 * SUB, SUB), jnp.float32),
            ],
        ),
        compiler_params=pltpu.CompilerParams(vmem_limit_bytes=SMALL_LIMIT),
        cost_estimate=pl.CostEstimate(
            flops=4 * 512 * 256 * slots, bytes_accessed=4 * SUB * slots, transcendentals=0
        ),
        name="residuals",
    )(count, *grid_parts, u_weights, v_weights, observed)


def adjoint_kernel(place, *refs):
    re_own, re_high, re_low, re_far_low, re_far_high = refs[:5]
    im_own, im_high, im_low, im_far_low, im_far_high = refs[5:10]
    base, left, right, kept, given, plane, im_all, left_mat, right_mat = refs[10:]
    step = pl.program_id(0)
    band_rows, cols = kept.shape[2:]

    @pl.when(step == 0)
    def _():
        plane[...] = jnp.zeros_like(plane)
        im_all[0] = im_own[...]
        im_all[1] = im_high[...]
        im_all[2] = im_low[...]
        im_all[3, :, :HALF] = im_far_low[...]
        im_all[3, :, HALF:] = im_far_high[...]
        a_re, a_im = (x.astype(jnp.bfloat16) for x in transposed_table(base, left))
        left_mat[...] = stacked(side_by_side(a_re, a_im), side_by_side(-a_im, a_re))
        b_re, b_im = (x.T.astype(jnp.bfloat16) for x in transposed_table(base, right))
        right_mat[...] = stacked(side_by_side(b_re, -b_im), side_by_side(b_im, b_re))

    re_blocks = (re_own[0], re_high[0], re_low[0], stacked(re_far_low[0], re_far_high[0]))
    edge = jnp.zeros((MC, LANES), jnp.float32)
    halves = []
    for other in range(RING):
        grid = stacked(re_blocks[other], im_all[step, other])
        half = f32_dot(left_mat[...], grid).astype(jnp.bfloat16)
        halves.append(side_by_side(half[:MC], half[MC:]))
    wholes = f32_dot(stacked(*halves), right_mat[...])
    for other in range(RING):
        source = step * RING + other
        top = pl.multiple_of(place[2 + 2 * source] * STEP, STEP)
        left_col = place[3 + 2 * source]
        odd = left_col // STEP % 2
        col = pl.multiple_of(left_col // LANES * LANES, LANES)
        for part in range(2):
            whole = wholes[other * MC : (other + 1) * MC, part * MC : (part + 1) * MC]
            wide = pltpu.roll(side_by_side(whole, edge), odd * STEP, 1)
            plane[part, pl.ds(top, MC), pl.ds(col, MC + LANES)] += wide

    @pl.when(step == RING - 1)
    def _():
        for group, out in enumerate((kept, given)):
            for near in range(RING):
                band = place[2 + 2 * RING * RING + RING * group + near]
                first = pl.multiple_of(band * band_rows, 8)
                for part in range(2):
                    rows = plane[part, pl.ds(first, band_rows), :]
                    out[near, part] = rows[:, :cols].astype(jnp.bfloat16)


def adjoint_plane(place, re_parts, im_parts, base, phases, bands, rows, cols):
    facets = phases.shape[0]
    flops = facets * 2 * 2 * 512 * 512 * 256
    wide = (cols + LANES - 1) // LANES * LANES
    band_shape = (RING, 2, rows // bands, cols)
    stepped = [pl.BlockSpec((1,) + x.shape[1:], lambda t, place: (t, 0, 0)) for x in re_parts]
    whole = [pl.BlockSpec(x.shape, lambda t, place: (0, 0, 0)) for x in im_parts]
    return pl.pallas_call(
        adjoint_kernel,
        out_shape=(jax.ShapeDtypeStruct(band_shape, jnp.bfloat16),) * 2,
        grid_spec=pltpu.PrefetchScalarGridSpec(
            num_scalar_prefetch=1,
            grid=(RING,),
            in_specs=stepped
            + whole
            + [
                pl.BlockSpec((2, MC, SUB), lambda t, place: (0, 0, 0)),
                pl.BlockSpec((1, 2, SUB), lambda t, place: (place[0], 0, 0)),
                pl.BlockSpec((1, 2, SUB), lambda t, place: (place[1], 0, 0)),
            ],
            out_specs=(pl.BlockSpec(band_shape, lambda t, place: (0, 0, 0, 0)),) * 2,
            scratch_shapes=[
                pltpu.VMEM((2, rows, wide), jnp.float32),
                pltpu.VMEM((RING, RING, SUB, SUB), jnp.bfloat16),
                pltpu.VMEM((2 * MC, 2 * SUB), jnp.bfloat16),
                pltpu.VMEM((2 * SUB, 2 * MC), jnp.bfloat16),
            ],
        ),
        compiler_params=pltpu.CompilerParams(vmem_limit_bytes=SMALL_LIMIT),
        cost_estimate=pl.CostEstimate(flops=flops, bytes_accessed=8 * MIB, transcendentals=0),
        name="adjoint_plane",
    )(place, *re_parts, *im_parts, base, phases, phases)


def along_x(shift):
    return "facet", [(i, (i // RING + shift) % RING * RING + i % RING) for i in range(RING * RING)]


def along_y(shift):
    return "facet", [(i, i // RING * RING + (i % RING + shift) % RING) for i in range(RING * RING)]


def along_z(shift):
    return "sub", [(i, (i // 2 + shift) % RING * 2 + i % 2) for i in range(2 * RING)]


def move(value, route):
    return lax.ppermute(value, *route)


def with_rows(block, rows, first):
    space = [(0, 0, 0)] * block.ndim
    space[-2] = (first, block.shape[-2] - rows.shape[-2] - first, 0)
    return block + lax.pad(rows, jnp.zeros((), rows.dtype), space)


def send_far(far_up, far_down, route):
    return move(far_up, route(1)), move(far_down, route(-1))


def send_near(up, down, arrived, route):
    low, high = arrived
    return move(with_rows(up, low, 0), route(1)), move(with_rows(down, high, HALF), route(-1))


def reduce_small(blocks, routes):
    return [
        (block[:1],)
        + tuple(move(block[k : k + 1], route(NEAR[k])) for k in range(1, RING))
        for block, route in zip(blocks, routes)
    ]


def gather_rings(blocks, routes):
    parts = []
    for block, route in zip(blocks, routes):
        low, high = move(block, route(1)), move(block, route(-1))
        far = (move(low[:, :HALF], route(1)), move(high[:, HALF:], route(-1)))
        parts.append((block, high, low) + far)
    return parts


def in_one(parts):
    own, high, low, far_low, far_high = parts
    return jnp.concatenate([own, high, low, jnp.concatenate([far_low, far_high], axis=1)], axis=0)


def sum_rings(kept, given):
    swapped = lax.ppermute(given, "sub", [(i, i ^ 1) for i in range(2 * RING)])
    chip = kept + swapped
    low = move(chip[3, 0], along_z(1))
    high = move(chip[3, 1], along_z(-1))
    up_im = move(chip[1, 1], along_z(1))
    down_re = move(chip[2, 0], along_z(-1))
    up_re = move(chip[1, 0] + low, along_z(1))
    down_im = move(chip[2, 1] + high, along_z(-1))
    own = kept[0].astype(jnp.float32) + swapped[0].astype(jnp.float32)
    re = own[0] + up_re.astype(jnp.float32) + down_re.astype(jnp.float32)
    im = own[1] + up_im.astype(jnp.float32) + down_im.astype(jnp.float32)
    return jnp.stack([re, im])


def on_device(facet_spec, worker_of_subgrid, vis_count, bin_offsets, bin_fractions, observed):
    subs = lax.axis_size("sub")
    rows, cols = facet_spec.shape[2:]
    base, phases = (jnp.asarray(x) for x in phase_parts(lax.axis_size("facet")))
    routes = (along_x, along_y)
    spec = jnp.swapaxes(facet_spec, 2, 3)
    part, most = (RING, HALF, SUB), (FAR, SUB, SUB)
    *outs, place = far_parts(worker_of_subgrid, spec, base, phases, (part,) * 4 + (most,) * 2)
    arrived = [send_far(*outs[:2], along_x), send_far(*outs[2:4], along_y)]
    nears = near_parts(place, spec, base, phases, (most,) * 6)
    arrived, nears, bin_offsets = lax.optimization_barrier((arrived, nears, bin_offsets))
    nears = [
        jnp.concatenate([block, outs[4 + k // 3][k % 3][None]]) for k, block in enumerate(nears)
    ]
    weights = kernel_weights(bin_offsets, bin_fractions)
    sums = [
        (own,) + send_near(up, down, got, route)
        for (own, up, down), got, route in zip((nears[:3], nears[3:]), arrived, routes)
    ]
    (own, weights) = lax.optimization_barrier((sums[0][0], weights))
    sums[0] = (own,) + sums[0][1:]
    wide = [sum(x.astype(jnp.float32) for x in parts) for parts in sums]
    sums = reduce_small([x.astype(jnp.bfloat16) for x in wide], routes[::-1])
    residual, re_part, im_part = residuals(
        vis_count, sums[0] + sums[1], *weights, observed
    )
    gathered = gather_rings((re_part, im_part), routes)
    gathered = gather_rings([in_one(parts) for parts in gathered], routes[::-1])
    kept, given = adjoint_plane(
        place, gathered[0], gathered[1], base, phases, subs, rows, cols
    )
    update = sum_rings(kept, given)
    return (residual, update[None])


def solution(mesh):
    placed = (
        P("facet", None, None, None),
        P(),
        P(("facet", "sub")),
        P(("facet", "sub"), None, None),
        P(("facet", "sub"), None, None),
        P(("facet", "sub"), None, None),
    )
    return jax.shard_map(
        on_device,
        mesh=mesh,
        in_specs=placed,
        out_specs=(P(("facet", "sub"), None, None), P("facet", None, "sub", None)),
        check_vma=False,
    )
```
